512 devices in a mesh: row: 32 (over z, x_lo), col: 16 (over x_hi, y, core).
Axes of the slice: x: 4 (x_hi: 2, x_lo: 2; x = x_hi * 2 + x_lo), y: 4, z: 16, core: 2. Of those that a mesh axis runs over, the one named last changes fastest.
Arguments:
- image: bfloat16 [256, 256, 256], P('row', 'col'), may hold values from -6 to 6
- w_qkv: bfloat16 [256, 768], replicated, may hold values from -0.375 to 0.375
- w_out: bfloat16 [256, 256], replicated, may hold values from -0.375 to 0.375
- norm_gain: float32 [256], replicated, may hold values from 0.25 to 1.75
- head_scale: float32 [4], replicated, may hold values from 4 to 12
- cotangent: bfloat16 [256, 256, 256], P('row', 'col'), may hold values from -6 to 6
Outputs:
- output: bfloat16 [256, 256, 256], P('row', 'col')
- grad_image: bfloat16 [256, 256, 256], P('row', 'col')
- grad_qkv: float32 [256, 768], replicated
- grad_out: float32 [256, 256], replicated
- grad_gain: float32 [256], replicated
- grad_scale: float32 [4], replicated
The draws below stay inside these ranges and needn't reach their ends.
All inputs are finite; a program needn't handle non-finite values.
Results may differ from the reference program's by a relative error of at most 0.0093.
Values may be sent and summed in bfloat16 or wider, within the bound.
A program may use at most 64 MiB of HBM per device.

```python
import math
import jax
import jax.numpy as jnp
from jax import lax

C = 256
HEADS = 4
HEAD_DIM = 64
RADIUS = 3
TH = 8
TW = 16
H = 256
W = 256


def levels(rng, dims, pieces, least, largest):
    factor_of = 1.0
    for position, parts in pieces:
        draws = jax.random.uniform(jax.random.fold_in(jax.random.fold_in(rng, 6), position), (parts,), jnp.float32, least / len(pieces), largest / len(pieces))
        factor_of = factor_of * jnp.repeat(jnp.exp(draws), dims[position] // parts).reshape((-1,) + (1,) * (len(dims) - 1 - position))
    return factor_of


def centred(rng, extent, scale, most, pieces=(), kind=jnp.bfloat16):
    drawn = scale * jax.random.normal(rng, extent, jnp.float32)
    if pieces:
        drawn = drawn * levels(rng, extent, pieces, -0.22, 0.18)
    return jnp.clip(drawn, -most, most).astype(kind)


def setup_inputs(seed: int = 0) -> dict:
    key_of = jax.random.split(jax.random.key(seed), 7)
    return {
        "image": centred(key_of[0], (H, W, C), 1.0, 6.0, ((0, 32), (1, 16))),
        "w_qkv": centred(key_of[1], (C, 3 * C), C ** -0.5, 0.375),
        "w_out": centred(key_of[2], (C, C), C ** -0.5, 0.375),
        "norm_gain": jnp.clip(1.0 + 0.15 * jax.random.normal(key_of[3], (C,), jnp.float32), 0.25, 1.75),
        "head_scale": jnp.clip(jnp.exp(jax.random.uniform(key_of[4], (HEADS,), jnp.float32, math.log(4.0), math.log(12.0))), 4.0, 12.0),
        "cotangent": centred(key_of[5], (H, W, C), 1.0, 6.0, ((0, 32), (1, 16))),
    }


EPS_NORM = 1e-06
EPS_UNIT = 1e-06

def rms_norm(values, norm_gain):
    inverse = lax.rsqrt(lax.optimization_barrier(jnp.mean(values * values, axis=-1, keepdims=True)) + EPS_NORM)
    return values * inverse * norm_gain

def unit_heads(values):
    per_head = values.reshape(values.shape[:-1] + (HEADS, HEAD_DIM))
    inverse = lax.rsqrt(lax.optimization_barrier(jnp.sum(per_head * per_head, axis=-1, keepdims=True)) + EPS_UNIT)
    return per_head * inverse

def attend(packed, scales, inside):
    query_rows = packed.shape[0] - 2 * RADIUS
    query_cols = packed.shape[1] - 2 * RADIUS
    query_unit = unit_heads(packed[RADIUS:RADIUS + query_rows, RADIUS:RADIUS + query_cols, :C])
    key_unit = unit_heads(packed[:, :, C:2 * C])
    value_heads = packed[:, :, 2 * C:].reshape(packed.shape[:2] + (HEADS, HEAD_DIM))
    weight_total = jnp.zeros((query_rows, query_cols, HEADS), jnp.float32)
    weighted_sum = jnp.zeros((query_rows, query_cols, HEADS, HEAD_DIM), jnp.float32)
    for shift_row in range(2 * RADIUS + 1):
        for shift_col in range(2 * RADIUS + 1):
            key_block = key_unit[shift_row:shift_row + query_rows, shift_col:shift_col + query_cols]
            value_block = value_heads[shift_row:shift_row + query_rows, shift_col:shift_col + query_cols]
            inside_block = inside[shift_row:shift_row + query_rows, shift_col:shift_col + query_cols]
            weight = jnp.exp(scales * lax.optimization_barrier(jnp.sum(query_unit * key_block, axis=-1))) * inside_block[:, :, None]
            weight_total = weight_total + weight
            weighted_sum = weighted_sum + weight[..., None] * value_block
    return (weighted_sum / weight_total[..., None]).reshape(query_rows, query_cols, C)

def reference(image, w_qkv, w_out, norm_gain, head_scale, cotangent):
    tiles_down = H // TH
    tiles_across = W // TW
    zero_index = jnp.zeros((), jnp.int32)
    padded_image = jnp.pad(image, ((2 * RADIUS, 2 * RADIUS), (2 * RADIUS, 2 * RADIUS), (0, 0)))
    padded_grad = jnp.pad(cotangent, ((RADIUS, RADIUS), (RADIUS, RADIUS), (0, 0)))

    def one_tile(carry, tile_index):
        tile_row = tile_index // tiles_across
        tile_col = tile_index % tiles_across
        top_edge = tile_row * TH
        left_edge = tile_col * TW
        extended = lax.dynamic_slice(padded_image, (top_edge, left_edge, zero_index), (TH + 4 * RADIUS, TW + 4 * RADIUS, C))
        normed = rms_norm(extended.astype(jnp.float32), norm_gain).astype(jnp.bfloat16)
        packed = jnp.dot(normed, w_qkv, preferred_element_type=jnp.float32).astype(jnp.bfloat16)
        row_ids = top_edge - 2 * RADIUS + jnp.arange(TH + 4 * RADIUS, dtype=jnp.int32)
        col_ids = left_edge - 2 * RADIUS + jnp.arange(TW + 4 * RADIUS, dtype=jnp.int32)
        row_ok = (row_ids >= 0) & (row_ids < H)
        col_ok = (col_ids >= 0) & (col_ids < W)
        inside = (row_ok[:, None] & col_ok[None, :]).astype(jnp.float32)
        scale_grid = jnp.broadcast_to(head_scale, (TH + 2 * RADIUS, TW + 2 * RADIUS, HEADS))
        attended, pullback = jax.vjp(lambda packed_float, scale_float: attend(packed_float, scale_float, inside), packed.astype(jnp.float32), scale_grid)
        mixed = attended.astype(jnp.bfloat16)
        grad_ext = lax.dynamic_slice(padded_grad, (top_edge, left_edge, zero_index), (TH + 2 * RADIUS, TW + 2 * RADIUS, C))
        grad_mixed = jnp.dot(grad_ext, w_out.T, preferred_element_type=jnp.float32)
        grad_packed, grad_scale_grid = pullback(grad_mixed)
        grad_tile = grad_packed[2 * RADIUS:2 * RADIUS + TH, 2 * RADIUS:2 * RADIUS + TW].astype(jnp.bfloat16)
        mixed_own = mixed[RADIUS:RADIUS + TH, RADIUS:RADIUS + TW]
        image_own = extended[2 * RADIUS:2 * RADIUS + TH, 2 * RADIUS:2 * RADIUS + TW].astype(jnp.float32)
        normed_own = normed[2 * RADIUS:2 * RADIUS + TH, 2 * RADIUS:2 * RADIUS + TW]
        grad_own = grad_ext[RADIUS:RADIUS + TH, RADIUS:RADIUS + TW]
        output_tile = (image_own + jnp.dot(mixed_own, w_out, preferred_element_type=jnp.float32)).astype(jnp.bfloat16)
        out_term = jnp.dot(mixed_own.reshape(-1, C).T, grad_own.reshape(-1, C), preferred_element_type=jnp.float32)
        qkv_term = jnp.dot(normed_own.reshape(-1, C).T, grad_tile.reshape(-1, 3 * C), preferred_element_type=jnp.float32)
        grad_normed = jnp.dot(grad_tile, w_qkv.T, preferred_element_type=jnp.float32)
        normed_value, norm_pull = jax.vjp(rms_norm, image_own, norm_gain)
        grad_image_norm, gain_term = norm_pull(grad_normed)
        grad_image_tile = (grad_own.astype(jnp.float32) + grad_image_norm).astype(jnp.bfloat16)
        scale_term = lax.optimization_barrier(jnp.sum(grad_scale_grid[RADIUS:RADIUS + TH, RADIUS:RADIUS + TW], axis=(0, 1)))
        totals = (carry[0] + qkv_term, carry[1] + out_term, carry[2] + gain_term, carry[3] + scale_term)
        return (totals, (output_tile, grad_image_tile))
    start = (jnp.zeros((C, 3 * C), jnp.float32), jnp.zeros((C, C), jnp.float32), jnp.zeros((C,), jnp.float32), jnp.zeros((HEADS,), jnp.float32))
    totals, stacked = lax.scan(one_tile, start, jnp.arange(tiles_down * tiles_across, dtype=jnp.int32))

    def assemble(tiles):
        return tiles.reshape(tiles_down, tiles_across, TH, TW, C).transpose(0, 2, 1, 3, 4).reshape(H, W, C)
    factor = 1.0 / math.sqrt(H * W)
    return (assemble(stacked[0]), assemble(stacked[1]), totals[0] * factor, totals[1] * factor, totals[2] * factor, totals[3] * factor)
```

```python
import math

import jax
import jax.numpy as jnp
from jax import lax
from jax.experimental import pallas as pl
from jax.experimental.pallas import tpu as pltpu
from jax.sharding import PartitionSpec as P

C = 256
HEADS = 4
HEAD_DIM = 64
RADIUS = 3
TH = 8
TW = 16
OWN = TH * TW
HALO = 224
KEYS = OWN + HALO
LANES = HEADS * OWN
EPS = 1e-06
NP = 16
NZ = 16
MESH = pl.DeviceIdType.MESH
F32 = jnp.float32
BF16 = jnp.bfloat16

PLACES = (
    (0, 48, -3, 0, 16),
    (48, 48, TH, 0, 16),
    (96, 32, 0, -3, 4),
    (128, 32, 0, TW, 4),
    (160, 16, -3, -3, 4),
    (176, 16, -3, TW, 4),
    (192, 16, TH, -3, 4),
    (208, 16, TH, TW, 4),
)
OWNERS = ((-1, 0), (1, 0), (0, -1), (0, 1), (-1, -1), (-1, 1), (1, -1), (1, 1))


def dot(a, b, contract=((1,), (0,))):
    return lax.dot_general(a, b, (contract, ((), ())), preferred_element_type=F32)


def key_mask(row, col, height, breadth):
    blocks = []
    for first, count, y0, x0, across in ((-1, OWN, 0, 0, TW),) + PLACES:
        place = lax.broadcasted_iota(jnp.int32, (count, OWN), 0)
        query = lax.broadcasted_iota(jnp.int32, (count, OWN), 1)
        y = place // across + y0
        x = place % across + x0
        ok = (jnp.abs(y - query // TW) <= RADIUS) & (jnp.abs(x - query % TW) <= RADIUS)
        gy = y + row * TH
        gx = x + col * TW
        ok = ok & (gy >= 0) & (gy < height) & (gx >= 0) & (gx < breadth)
        if across == 4:
            ok = ok & (place % 4 < RADIUS)
            if count == 16:
                ok = ok & (place // 4 < RADIUS)
        blocks.append(jnp.where(ok, 1.0, 0.0).astype(F32))
    return jnp.concatenate(blocks, axis=0)


def selection():
    blocks = []
    for first, count, y0, x0, across in PLACES[2:]:
        place = lax.broadcasted_iota(jnp.int32, (count, OWN), 0)
        pixel = lax.broadcasted_iota(jnp.int32, (count, OWN), 1)
        y = place // 4 + (y0 + TH) % TH
        x = place % 4 + (x0 + TW) % TW
        ok = (pixel == y * TW + x) & (place % 4 < RADIUS)
        if count == 16:
            ok = ok & (place // 4 < RADIUS)
        blocks.append(jnp.where(ok, 1.0, 0.0).astype(F32))
    return jnp.concatenate(blocks, axis=0).astype(BF16)


def block(
    rows,
    cols,
    factor,
    image_ref,
    w_qkv_ref,
    w_out_ref,
    gain_ref,
    scale_ref,
    cot_ref,
    output_ref,
    grad_image_ref,
    grad_qkv_ref,
    grad_out_ref,
    grad_gain_ref,
    grad_scale_ref,
    halo,
    side,
    grad_send,
    grad_back,
    q_block,
    g_block,
    total,
    send0,
    recv0,
    mine,
    small0,
    small0r,
    small1,
    send1,
    recv1,
    send2,
    recv2,
    recv3,
    gathered,
    sems,
):
    row = lax.axis_index("row")
    col = lax.axis_index("col")
    z = row // 2
    core = col % 2
    chip = (row % 2) * 8 + col // 2
    sibling = (row, col + 1 - 2 * core)

    def chip_id(other):
        return (z * 2 + other // 8, (other % 8) * 2 + core)

    def z_id(other):
        return (other * 2 + row % 2, col)

    def neighbour(step):
        return (lax.rem(row + step[0] + rows, rows), lax.rem(col + step[1] + cols, cols))

    barrier = pltpu.get_barrier_semaphore()
    for step in OWNERS:
        pl.semaphore_signal(barrier, inc=1, device_id=neighbour(step), device_id_type=MESH)
    pl.semaphore_signal(barrier, inc=1, device_id=sibling, device_id_type=MESH)

    def greet(k, carry):
        pl.semaphore_signal(
            barrier, inc=1, device_id=chip_id(lax.rem(chip + k, NP)), device_id_type=MESH
        )
        pl.semaphore_signal(
            barrier, inc=1, device_id=z_id(lax.rem(z + k, NZ)), device_id_type=MESH
        )
        return carry

    lax.fori_loop(1, NP, greet, 0)

    def remote(src, dst, sem, device):
        return pltpu.make_async_remote_copy(
            src_ref=src,
            dst_ref=dst,
            send_sem=sems.at[2 * sem],
            recv_sem=sems.at[2 * sem + 1],
            device_id=device,
            device_id_type=MESH,
        )

    def wait_sent(ref, sem):
        pltpu.make_async_copy(ref, ref, sems.at[2 * sem]).wait()

    def wait_received(ref, sem):
        pltpu.make_async_copy(ref, ref, sems.at[2 * sem + 1]).wait()

    sel = selection()
    side[...] = dot(sel, image_ref[...]).astype(BF16)

    pl.semaphore_wait(barrier, 8 + 1 + (NP - 1) + (NZ - 1))

    for place, step in zip(PLACES, OWNERS):
        first, count = place[0], place[1]
        if first == 0:
            src = image_ref.at[pl.ds(OWN - 48, 48)]
        elif first == 48:
            src = image_ref.at[pl.ds(0, 48)]
        else:
            src = side.at[pl.ds(first - 96, count)]
        remote(
            src, halo.at[pl.ds(first, count)], 0, neighbour((-step[0], -step[1]))
        ).start()

    gain = gain_ref[...]
    w_q = w_qkv_ref[:, :C]
    w_kv = w_qkv_ref[:, C:]
    cot = cot_ref[...]
    mask = key_mask(row, col, rows * TH, cols * TW)

    def norm(values):
        inverse = lax.rsqrt(jnp.mean(values * values, axis=-1, keepdims=True) + EPS)
        return inverse, (values * inverse * gain).astype(BF16)

    own_float = image_ref[...].astype(F32)
    own_inverse, own_normed = norm(own_float)
    own_normed_t = own_normed.astype(F32).T.astype(BF16)
    query = dot(own_normed, w_q).astype(BF16)
    query_t = query.astype(F32).T
    q_block[...] = jnp.zeros_like(q_block)
    g_block[...] = jnp.zeros_like(g_block)
    grad_mixed_t = dot(w_out_ref[...], cot, ((1,), (1,)))
    q_inverse = []
    for h in range(HEADS):
        ch = slice(h * HEAD_DIM, (h + 1) * HEAD_DIM)
        ln = slice(h * OWN, (h + 1) * OWN)
        part = query_t[ch]
        q_block[ch, ln] = part.astype(BF16)
        g_block[ch, ln] = grad_mixed_t[ch].astype(BF16)
        q_inverse.append(lax.rsqrt(jnp.sum(part * part, axis=0, keepdims=True) + EPS))
    own_kv = dot(own_normed, w_kv)

    wait_sent(halo, 0)
    wait_received(halo, 0)

    halo_float = halo[...].astype(F32)
    halo_inverse, halo_normed = norm(halo_float)
    halo_normed_t = halo_normed.astype(F32).T.astype(BF16)
    halo_kv = dot(halo_normed, w_kv)
    kv = jnp.concatenate([own_kv, halo_kv], axis=0).astype(BF16)
    keys = kv[:, :C]
    values = kv[:, C:]
    keys_float = keys.astype(F32)
    keys_t = keys_float.T.astype(BF16)
    values_t = values.astype(F32).T.astype(BF16)

    scores = dot(keys, q_block[...])
    grad_probs = dot(values, g_block[...])
    probs = []
    grad_logits = []
    k_inverse = []
    k_along = []
    attended_t = []
    grad_q_t = []
    scale_sum = jnp.zeros((1, OWN), F32)
    lane = lax.broadcasted_iota(jnp.int32, (1, OWN), 1)
    for h in range(HEADS):
        ch = slice(h * HEAD_DIM, (h + 1) * HEAD_DIM)
        ln = slice(h * OWN, (h + 1) * OWN)
        k_part = keys_float[:, ch]
        k_inv = lax.rsqrt(jnp.sum(k_part * k_part, axis=1, keepdims=True) + EPS)
        scale = scale_ref[h]
        logit = scores[:, ln] * k_inv * (q_inverse[h] * scale)
        weight = jnp.exp(logit) * mask
        prob = weight * (1.0 / jnp.sum(weight, axis=0, keepdims=True))
        prob_bf = prob.astype(BF16)
        probs.append(prob_bf)
        attended_t.append(dot(values_t[ch], prob_bf))
        grad_prob = grad_probs[:, ln]
        row_dot = jnp.sum(prob * grad_prob, axis=0, keepdims=True)
        grad_logit = prob * (grad_prob - row_dot)
        product = grad_logit * logit
        along_q = jnp.sum(product, axis=0, keepdims=True)
        scale_sum = scale_sum + jnp.where(
            lane == h, jnp.sum(along_q, axis=1, keepdims=True) / scale, 0.0
        )
        k_along.append(jnp.sum(product, axis=1, keepdims=True))
        k_inverse.append(k_inv)
        grad_cos = grad_logit * scale
        grad_logits.append((grad_cos * q_inverse[h]).astype(BF16))
        unit_grad = dot(keys_t[ch], (grad_cos * k_inv).astype(BF16))
        grad_q_t.append(
            q_inverse[h] * (unit_grad - query_t[ch] * (q_inverse[h] * along_q))
        )

    attended_t = jnp.concatenate(attended_t, axis=0)
    mixed_t = attended_t.astype(BF16)
    mixed = attended_t.T.astype(BF16)
    output_ref[...] = (own_float + dot(mixed, w_out_ref[...])).astype(BF16)
    total[pl.ds(3 * C, C), :] = dot(mixed_t, cot)

    grad_q = jnp.concatenate(grad_q_t, axis=0).T.astype(BF16)
    grad_k_unit = dot(jnp.concatenate(grad_logits, axis=1), q_block[...], ((1,), (1,)))
    grad_v = dot(jnp.concatenate(probs, axis=1), g_block[...], ((1,), (1,))).astype(BF16)
    low = lax.broadcasted_iota(jnp.int32, (1, OWN), 1) < HEAD_DIM
    grad_k = []
    for t in range(2):
        ln = slice(t * OWN, (t + 1) * OWN)
        inv = jnp.where(low, k_inverse[2 * t], k_inverse[2 * t + 1])
        along = jnp.where(low, k_along[2 * t], k_along[2 * t + 1])
        grad_k.append(inv * (grad_k_unit[:, ln] - keys_float[:, ln] * (inv * along)))
    grad_k = jnp.concatenate(grad_k, axis=1).astype(BF16)
    grad_kv = jnp.concatenate([grad_k, grad_v], axis=1)

    total[pl.ds(0, C), :] = dot(own_normed_t, grad_q)
    normed_t = jnp.concatenate([own_normed_t, halo_normed_t], axis=1)
    kv_term = dot(normed_t, grad_kv)
    total[pl.ds(C, C), :] = kv_term[:, :C]
    total[pl.ds(2 * C, C), :] = kv_term[:, C:]

    half = pl.multiple_of((1 - core) * 512, 512)
    kept = pl.multiple_of(core * 512, 512)
    send0[...] = total[pl.ds(half, 512), :].astype(BF16)
    remote(send0, recv0, 1, sibling).start()

    grad_normed = dot(grad_kv, w_kv, ((1,), (1,)))
    grad_normed_own = grad_normed[:OWN] + dot(grad_q, w_q, ((1,), (1,)))

    def norm_back(values, inverse, grad):
        scaled = values * inverse
        gain_term = jnp.sum(grad * scaled, axis=0, keepdims=True)
        grad = grad * gain
        along = jnp.mean(grad * scaled, axis=-1, keepdims=True)
        return gain_term, inverse * (grad - scaled * along)

    gain_own, image_own = norm_back(own_float, own_inverse, grad_normed_own)
    gain_halo, image_halo = norm_back(halo_float, halo_inverse, grad_normed[OWN:])
    gain_sum = gain_own + gain_halo
    grad_send[...] = image_halo.astype(BF16)
    for place, step in zip(PLACES, OWNERS):
        there = pl.ds(place[0], place[1])
        remote(grad_send.at[there], grad_back.at[there], 2, neighbour(step)).start()

    small0[...] = jnp.concatenate(
        [scale_sum, gain_sum[:, :OWN], gain_sum[:, OWN:], jnp.zeros((5, OWN), F32)], axis=0
    )
    remote(small0, small0r, 3, sibling).start()

    wait_received(recv0, 1)
    mine[...] = total[pl.ds(kept, 512), :] + recv0[...].astype(F32)
    send1[...] = mine[...].astype(BF16)

    def chunk(other):
        return pl.ds(pl.multiple_of(other * 32, 32), 32)

    def scatter1(k, carry):
        other = lax.rem(chip + k, NP)
        remote(send1.at[chunk(other)], recv1.at[chunk(k - 1)], 4, chip_id(other)).start()
        return carry

    lax.fori_loop(1, NP, scatter1, 0)
    wait_received(small0r, 3)
    small1[chip] = small0[...] + small0r[...]

    def scatter1s(k, carry):
        other = lax.rem(chip + k, NP)
        remote(small1.at[chip], small1.at[chip], 5, chip_id(other)).start()
        return carry

    lax.fori_loop(1, NP, scatter1s, 0)

    wait_received(grad_back, 2)
    grad_image = cot.astype(F32) + image_own
    grad_image = grad_image + dot(sel, grad_back[pl.ds(96, 128), :], ((0,), (0,)))
    top = grad_back[pl.ds(48, 48), :].astype(F32)
    bottom = grad_back[pl.ds(0, 48), :].astype(F32)
    grad_image = jnp.concatenate(
        [grad_image[:48] + top, grad_image[48:80], grad_image[80:] + bottom], axis=0
    )
    grad_image_ref[...] = grad_image.astype(BF16)

    wait_received(recv1.at[pl.ds(0, 15 * 32)], 4)
    summed = mine[chunk(chip), :]
    for k in range(NP - 1):
        summed = summed + recv1[pl.ds(k * 32, 32), :].astype(F32)
    wait_received(small1.at[pl.ds(0, 15)], 5)
    small = small1[0]
    for k in range(1, NP):
        small = small + small1[k]

    for i in range(NZ):
        a, b, c = i // 4, (i // 2) % 2, i % 2
        send2[i] = jnp.concatenate(
            [summed[8 * a + 4 * c : 8 * a + 4 * c + 4, 128 * b : 128 * b + 128], small[:4]],
            axis=0,
        )
    recv2[z] = send2[z]

    def scatter2(k, carry):
        other = lax.rem(z + k, NZ)
        remote(send2.at[other], recv2.at[z], 6, z_id(other)).start()
        return carry

    lax.fori_loop(1, NZ, scatter2, 0)
    wait_received(recv2.at[pl.ds(0, 15)], 6)
    piece = recv2[0]
    for k in range(1, NZ):
        piece = piece + recv2[k]
    piece = piece * factor
    grad_scale_ref[...] = piece[4:5]
    grad_gain_ref[...] = jnp.concatenate([piece[5:6], piece[6:7]], axis=1)
    recv3[z] = piece

    def gather3(k, carry):
        other = lax.rem(z + k, NZ)
        remote(recv3.at[z], recv3.at[z], 7, z_id(other)).start()
        return carry

    lax.fori_loop(1, NZ, gather3, 0)
    wait_received(recv3.at[pl.ds(0, 15)], 7)
    lines = []
    for a in range(4):
        lines.append(
            jnp.concatenate(
                [
                    jnp.concatenate([recv3[4 * a + 2 * b + c, :4] for c in range(2)], axis=0)
                    for b in range(2)
                ],
                axis=1,
            )
        )
    here = pl.multiple_of(core * 512 + chip * 32, 32)
    gathered[pl.ds(here, 32), :] = jnp.concatenate(lines, axis=0).astype(BF16)

    def gather4(k, carry):
        other = lax.rem(chip + k, NP)
        spot = gathered.at[pl.ds(here, 32)]
        remote(spot, spot, 8, chip_id(other)).start()
        return carry

    lax.fori_loop(1, NP, gather4, 0)
    wait_received(gathered.at[pl.ds(0, 15 * 32)], 8)
    mine_half = gathered.at[pl.ds(kept, 512)]
    remote(mine_half, mine_half, 9, sibling).start()
    wait_received(mine_half, 9)

    for j in range(3):
        grad_qkv_ref[:, pl.ds(j * C, C)] = gathered[pl.ds(j * C, C), :].astype(F32)
    grad_out_ref[...] = gathered[pl.ds(3 * C, C), :].astype(F32)

    wait_sent(send0, 1)
    wait_sent(grad_send, 2)
    wait_sent(small0, 3)
    wait_sent(recv1.at[pl.ds(0, 15 * 32)], 4)
    wait_sent(small1.at[pl.ds(0, 15)], 5)
    wait_sent(send2.at[pl.ds(0, 15)], 6)
    wait_sent(recv3.at[pl.ds(0, 15)], 7)
    wait_sent(gathered.at[pl.ds(0, 15 * 32)], 8)
    wait_sent(mine_half, 9)


def on_device(image, w_qkv, w_out, norm_gain, head_scale, cotangent):
    rows = lax.axis_size("row")
    cols = lax.axis_size("col")
    vmem = pl.BlockSpec(memory_space=pltpu.VMEM)
    smem = pl.BlockSpec(memory_space=pltpu.SMEM)
    factor = 1.0 / math.sqrt(rows * TH * cols * TW)

    def kernel(*refs):
        block(rows, cols, factor, *refs)

    output, grad_image, grad_qkv, grad_out, grad_gain, grad_scale = pl.pallas_call(
        kernel,
        out_shape=(
            jax.ShapeDtypeStruct((OWN, C), BF16),
            jax.ShapeDtypeStruct((OWN, C), BF16),
            jax.ShapeDtypeStruct((C, 3 * C), F32),
            jax.ShapeDtypeStruct((C, C), F32),
            jax.ShapeDtypeStruct((1, C), F32),
            jax.ShapeDtypeStruct((1, OWN), F32),
        ),
        in_specs=[vmem, vmem, vmem, vmem, smem, vmem],
        out_specs=(vmem,) * 6,
        scratch_shapes=[
            pltpu.VMEM((HALO, C), BF16),
            pltpu.VMEM((OWN, C), BF16),
            pltpu.VMEM((HALO, C), BF16),
            pltpu.VMEM((HALO, C), BF16),
            pltpu.VMEM((C, LANES), BF16),
            pltpu.VMEM((C, LANES), BF16),
            pltpu.VMEM((4 * C, C), F32),
            pltpu.VMEM((2 * C, C), BF16),
            pltpu.VMEM((2 * C, C), BF16),
            pltpu.VMEM((2 * C, C), F32),
            pltpu.VMEM((8, OWN), F32),
            pltpu.VMEM((8, OWN), F32),
            pltpu.VMEM((NP, 8, OWN), F32),
            pltpu.VMEM((2 * C, C), BF16),
            pltpu.VMEM((2 * C, C), BF16),
            pltpu.VMEM((NZ, 8, OWN), F32),
            pltpu.VMEM((NZ, 8, OWN), F32),
            pltpu.VMEM((NZ, 8, OWN), F32),
            pltpu.VMEM((4 * C, C), BF16),
            pltpu.SemaphoreType.DMA((20,)),
        ],
        compiler_params=pltpu.CompilerParams(
            collective_id=0, has_side_effects=True, vmem_limit_bytes=48 * 1024 * 1024
        ),
    )(
        image.reshape(OWN, C),
        w_qkv,
        w_out,
        norm_gain.reshape(1, C),
        head_scale,
        cotangent.reshape(OWN, C),
    )
    return (
        output.reshape(TH, TW, C),
        grad_image.reshape(TH, TW, C),
        grad_qkv,
        grad_out,
        grad_gain.reshape(C),
        grad_scale[0, :HEADS],
    )


def solution(mesh):
    placed = (P("row", "col", None), P(), P(), P(), P(), P("row", "col", None))
    return jax.shard_map(
        on_device,
        mesh=mesh,
        in_specs=placed,
        out_specs=(P("row", "col", None), P("row", "col", None), P(), P(), P(), P()),
        check_vma=False,
    )
```

```python
import math

import jax
import jax.numpy as jnp
from jax import lax
from jax.experimental import pallas as pl
from jax.experimental.pallas import tpu as pltpu
from jax.sharding import PartitionSpec as P

C = 256
HEADS = 4
HEAD_DIM = 64
RADIUS = 3
TH = 8
TW = 16
OWN = TH * TW
HALO = 224
KEYS = OWN + HALO
LANES = HEADS * OWN
EPS = 1e-06
NP = 16
VMEM_LIMIT = 60 * 1024 * 1024
NZ = 16
MESH = pl.DeviceIdType.MESH
F32 = jnp.float32
BF16 = jnp.bfloat16

PLACES = (
    (0, 48, -3, 0, 16),
    (48, 48, TH, 0, 16),
    (96, 32, 0, -3, 4),
    (128, 32, 0, TW, 4),
    (160, 16, -3, -3, 4),
    (176, 16, -3, TW, 4),
    (192, 16, TH, -3, 4),
    (208, 16, TH, TW, 4),
)
OWNERS = ((-1, 0), (1, 0), (0, -1), (0, 1), (-1, -1), (-1, 1), (1, -1), (1, 1))

STEPS = sorted(
    ((dx, dy) for dx in range(4) for dy in range(4) if dx or dy),
    key=lambda step: (-min(step[0], 4 - step[0]) - min(step[1], 4 - step[1]), step),
)
CAST_ORDER = (1, 2, 3, 4, 5, 15, 6, 14, 7, 13, 8, 12, 9, 11, 10)
HALO_SEM, BACK_SEM, SMALL_CORE, SMALL_PLANE, SMALL_LINE, SMALL_CAST, SMALL_GATHER = range(7)
CORE_SEM, PLANE_SEM, LINE_SEM, CAST_SEM, GATHER_SEM, BOTH_SEM = range(7, 19, 2)


def dot(a, b, contract=((1,), (0,))):
    return lax.dot_general(a, b, (contract, ((), ())), preferred_element_type=F32)


def key_mask(row, col, height, breadth):
    blocks = []
    for first, count, y0, x0, across in ((-1, OWN, 0, 0, TW),) + PLACES:
        place = lax.broadcasted_iota(jnp.int32, (count, OWN), 0)
        query = lax.broadcasted_iota(jnp.int32, (count, OWN), 1)
        y = place // across + y0
        x = place % across + x0
        ok = (jnp.abs(y - query // TW) <= RADIUS) & (jnp.abs(x - query % TW) <= RADIUS)
        gy = y + row * TH
        gx = x + col * TW
        ok = ok & (gy >= 0) & (gy < height) & (gx >= 0) & (gx < breadth)
        if across == 4:
            ok = ok & (place % 4 < RADIUS)
            if count == 16:
                ok = ok & (place // 4 < RADIUS)
        blocks.append(jnp.where(ok, 1.0, 0.0).astype(F32))
    return jnp.concatenate(blocks, axis=0)


def selection():
    blocks = []
    for first, count, y0, x0, across in PLACES[2:]:
        place = lax.broadcasted_iota(jnp.int32, (count, OWN), 0)
        pixel = lax.broadcasted_iota(jnp.int32, (count, OWN), 1)
        y = place // 4 + (y0 + TH) % TH
        x = place % 4 + (x0 + TW) % TW
        ok = (pixel == y * TW + x) & (place % 4 < RADIUS)
        if count == 16:
            ok = ok & (place // 4 < RADIUS)
        blocks.append(jnp.where(ok, 1.0, 0.0).astype(F32))
    return jnp.concatenate(blocks, axis=0).astype(BF16)


def block(rows, cols, factor, *refs):
    (
        image_hbm,
        w_qkv_hbm,
        w_out_hbm,
        gain_hbm,
        scale_ref,
        cot_hbm,
        output_hbm,
        grad_image_hbm,
        grad_qkv_hbm,
        grad_out_hbm,
        small_hbm,
        image_ref,
        w_qkv_ref,
        w_out_ref,
        gain_ref,
        cot_ref,
        halo,
        side,
        grad_send,
        grad_back,
        q_block,
        g_block,
        total,
        core_send,
        core_recv,
        mine,
        plane_send,
        plane_recv,
        line_send,
        line_recv,
        gathered,
        small_own,
        small_core,
        small_plane,
        small_line,
        small_total,
        output_ref,
        grad_image_ref,
        grad_qkv_ref,
        grad_out_ref,
        sems,
        local_sems,
    ) = refs
    row = lax.axis_index("row")
    col = lax.axis_index("col")
    z = row // 2
    core = col % 2
    x = (col // 8) * 2 + row % 2
    y = (col // 2) % 4
    chip = x * 4 + y
    sibling = (row, col + 1 - 2 * core)

    loads = []
    for i, (src, dst) in enumerate(
        (
            (image_hbm, image_ref),
            (w_qkv_hbm, w_qkv_ref),
            (cot_hbm, cot_ref),
            (w_out_hbm, w_out_ref),
            (gain_hbm, gain_ref),
        )
    ):
        load = pltpu.make_async_copy(src, dst, local_sems.at[i])
        load.start()
        loads.append(load)

    stores = []

    def store(src, dst):
        copy = pltpu.make_async_copy(src, dst, local_sems.at[len(loads) + len(stores)])
        copy.start()
        stores.append(copy)

    def chip_id(ox, oy):
        return (z * 2 + ox % 2, (ox // 2) * 8 + oy * 2 + core)

    def z_id(other):
        return (other * 2 + row % 2, col)

    def neighbour(step):
        return (lax.rem(row + step[0] + rows, rows), lax.rem(col + step[1] + cols, cols))

    peers = []
    for dx, dy in STEPS:
        ox, oy = lax.rem(x + dx, 4), lax.rem(y + dy, 4)
        peers.append((ox * 4 + oy, chip_id(ox, oy)))

    barrier = pltpu.get_barrier_semaphore()

    def greet(device):
        pl.semaphore_signal(barrier, inc=1, device_id=device, device_id_type=MESH)

    for step in OWNERS:
        greet(neighbour(step))
    for other, device in peers:
        greet(device)

    @pl.when(z != 0)
    def _():
        greet(z_id(0))

    @pl.when(z == 0)
    def _():
        for k in range(1, NZ):
            greet(z_id(k))

    def remote(src, dst, sem, device):
        return pltpu.make_async_remote_copy(
            src_ref=src,
            dst_ref=dst,
            send_sem=sems.at[2 * sem],
            recv_sem=sems.at[2 * sem + 1],
            device_id=device,
            device_id_type=MESH,
        )

    def wait_sent(ref, sem):
        pltpu.make_async_copy(ref, ref, sems.at[2 * sem]).wait()

    def wait_received(ref, sem):
        pltpu.make_async_copy(ref, ref, sems.at[2 * sem + 1]).wait()

    sel = selection()
    loads[0].wait()
    side[...] = dot(sel, image_ref[...]).astype(BF16)

    @pl.when(z != 0)
    def _():
        pl.semaphore_wait(barrier, 8 + (NP - 1) + 1)

    @pl.when(z == 0)
    def _():
        pl.semaphore_wait(barrier, 8 + (NP - 1) + (NZ - 1))

    for place, step in reversed(tuple(zip(PLACES, OWNERS))):
        first, count = place[0], place[1]
        if first == 0:
            src = image_ref.at[pl.ds(OWN - 48, 48)]
        elif first == 48:
            src = image_ref.at[pl.ds(0, 48)]
        else:
            src = side.at[pl.ds(first - 96, count)]
        remote(
            src, halo.at[pl.ds(first, count)], HALO_SEM, neighbour((-step[0], -step[1]))
        ).start()

    for load in loads[1:]:
        load.wait()
    gain = gain_ref[...]
    w_q = w_qkv_ref[:, :C]
    w_kv = w_qkv_ref[:, C:]
    cot = cot_ref[...]
    mask = key_mask(row, col, rows * TH, cols * TW)

    def norm(values):
        inverse = lax.rsqrt(jnp.mean(values * values, axis=-1, keepdims=True) + EPS)
        return inverse, (values * inverse * gain).astype(BF16)

    own_float = image_ref[...].astype(F32)
    own_inverse, own_normed = norm(own_float)
    own_normed_t = own_normed.astype(F32).T.astype(BF16)
    query = dot(own_normed, w_q).astype(BF16)
    query_t = query.astype(F32).T
    q_block[...] = jnp.zeros_like(q_block)
    g_block[...] = jnp.zeros_like(g_block)
    grad_mixed_t = dot(w_out_ref[...], cot, ((1,), (1,)))
    q_inverse = []
    for h in range(HEADS):
        ch = slice(h * HEAD_DIM, (h + 1) * HEAD_DIM)
        ln = slice(h * OWN, (h + 1) * OWN)
        part = query_t[ch]
        q_block[ch, ln] = part.astype(BF16)
        g_block[ch, ln] = grad_mixed_t[ch].astype(BF16)
        q_inverse.append(lax.rsqrt(jnp.sum(part * part, axis=0, keepdims=True) + EPS))
    own_kv = dot(own_normed, w_kv)

    wait_received(halo, HALO_SEM)

    halo_float = halo[...].astype(F32)
    halo_inverse, halo_normed = norm(halo_float)
    halo_normed_t = halo_normed.astype(F32).T.astype(BF16)
    halo_kv = dot(halo_normed, w_kv)
    kv = jnp.concatenate([own_kv, halo_kv], axis=0).astype(BF16)
    keys = kv[:, :C]
    values = kv[:, C:]
    keys_float = keys.astype(F32)
    values_t = values.astype(F32).T.astype(BF16)
    normed_t = jnp.concatenate([own_normed_t, halo_normed_t], axis=1)

    scores = dot(keys, q_block[...])
    probs = []
    probs_bf = []
    logits = []
    k_inverse = []
    attended_t = []
    for h in range(HEADS):
        ch = slice(h * HEAD_DIM, (h + 1) * HEAD_DIM)
        ln = slice(h * OWN, (h + 1) * OWN)
        k_part = keys_float[:, ch]
        k_inv = lax.rsqrt(jnp.sum(k_part * k_part, axis=1, keepdims=True) + EPS)
        logit = scores[:, ln] * k_inv * (q_inverse[h] * scale_ref[h])
        weight = jnp.exp(logit) * mask
        prob = weight * (1.0 / jnp.sum(weight, axis=0, keepdims=True))
        probs.append(prob)
        probs_bf.append(prob.astype(BF16))
        logits.append(logit)
        k_inverse.append(k_inv)
        attended_t.append(dot(values_t[ch], probs_bf[h]))
    attended_t = jnp.concatenate(attended_t, axis=0)
    grad_v = dot(jnp.concatenate(probs_bf, axis=1), g_block[...], ((1,), (1,))).astype(BF16)

    def start_core(stage):
        core_send[stage] = total[2 * stage + 1 - core].astype(BF16)
        remote(core_send.at[stage], core_recv.at[stage], CORE_SEM + stage, sibling).start()

    def start_plane(stage):
        wait_received(core_recv.at[stage], CORE_SEM + stage)
        summed = total[2 * stage + core] + core_recv[stage].astype(F32)
        mine[stage] = summed
        plane_send[stage] = summed.astype(BF16)
        for k, (other, device) in enumerate(peers):
            remote(
                plane_send.at[stage, pl.ds(pl.multiple_of(other * 16, 16), 16)],
                plane_recv.at[stage, k],
                PLANE_SEM + stage,
                device,
            ).start()

    def start_line(stage):
        fifteen = plane_recv.at[stage]
        wait_received(fifteen, PLANE_SEM + stage)
        summed = mine[stage, pl.ds(pl.multiple_of(chip * 16, 16), 16), :]
        for k in range(NP - 1):
            summed = summed + plane_recv[stage, k].astype(F32)

        @pl.when(z != 0)
        def _():
            line_send[stage] = summed.astype(BF16)
            remote(
                line_send.at[stage], line_recv.at[stage, z], LINE_SEM + stage, z_id(0)
            ).start()

        @pl.when(z == 0)
        def _():
            mine[stage, pl.ds(0, 16), :] = summed

    here = pl.ds(pl.multiple_of(chip * 16, 16), 16)

    def spot(stage):
        return gathered.at[2 * stage + core, here]

    def start_gather(stage):
        @pl.when(z == 0)
        def _():
            wait_received(line_recv.at[stage, pl.ds(1, NZ - 1)], LINE_SEM + stage)
            summed = mine[stage, pl.ds(0, 16), :]
            for k in range(1, NZ):
                summed = summed + line_recv[stage, k].astype(F32)
            gathered[2 * stage + core, here, :] = (summed * factor).astype(BF16)

        @pl.when(z != 0)
        def _():
            wait_received(spot(stage), CAST_SEM + stage)

        @pl.when(z == 0)
        def _():
            for k in CAST_ORDER[:4]:
                remote(spot(stage), spot(stage), CAST_SEM + stage, z_id(k)).start()

        for other, device in peers:
            remote(spot(stage), spot(stage), GATHER_SEM + stage, device).start()

        @pl.when(z == 0)
        def _():
            for k in CAST_ORDER[4:]:
                remote(spot(stage), spot(stage), CAST_SEM + stage, z_id(k)).start()

    def finish_gather(stage):
        own = gathered.at[2 * stage + core]
        wait_received(own.at[pl.ds(0, 240)], GATHER_SEM + stage)
        remote(own, own, BOTH_SEM + stage, sibling).start()

    mixed_t = attended_t.astype(BF16)
    total[0] = dot(normed_t, grad_v)
    total[1] = dot(mixed_t, cot)
    start_core(0)

    grad_probs = dot(values, g_block[...])
    keys_t = keys_float.T.astype(BF16)
    grad_logits = []
    k_along = []
    grad_q_t = []
    scale_sum = jnp.zeros((1, OWN), F32)
    lane = lax.broadcasted_iota(jnp.int32, (1, OWN), 1)
    for h in range(HEADS):
        ch = slice(h * HEAD_DIM, (h + 1) * HEAD_DIM)
        ln = slice(h * OWN, (h + 1) * OWN)
        scale = scale_ref[h]
        prob = probs[h]
        grad_prob = grad_probs[:, ln]
        row_dot = jnp.sum(prob * grad_prob, axis=0, keepdims=True)
        grad_logit = prob * (grad_prob - row_dot)
        product = grad_logit * logits[h]
        along_q = jnp.sum(product, axis=0, keepdims=True)
        scale_sum = scale_sum + jnp.where(
            lane == h, jnp.sum(along_q, axis=1, keepdims=True) / scale, 0.0
        )
        k_along.append(jnp.sum(product, axis=1, keepdims=True))
        grad_logits.append((grad_logit * (q_inverse[h] * scale)).astype(BF16))
        unit_grad = dot(keys_t[ch], (grad_logit * (k_inverse[h] * scale)).astype(BF16))
        grad_q_t.append(
            q_inverse[h] * (unit_grad - query_t[ch] * (q_inverse[h] * along_q))
        )

    grad_q = jnp.concatenate(grad_q_t, axis=0).T.astype(BF16)
    grad_k_unit = dot(jnp.concatenate(grad_logits, axis=1), q_block[...], ((1,), (1,)))
    low = lax.broadcasted_iota(jnp.int32, (1, OWN), 1) < HEAD_DIM
    grad_k = []
    for t in range(2):
        ln = slice(t * OWN, (t + 1) * OWN)
        inv = jnp.where(low, k_inverse[2 * t], k_inverse[2 * t + 1])
        along = jnp.where(low, k_along[2 * t], k_along[2 * t + 1])
        grad_k.append(inv * (grad_k_unit[:, ln] - keys_float[:, ln] * (inv * along)))
    grad_k = jnp.concatenate(grad_k, axis=1).astype(BF16)

    total[2] = dot(own_normed_t, grad_q)
    total[3] = dot(normed_t, grad_k)
    start_core(1)
    start_plane(0)

    grad_kv = jnp.concatenate([grad_k, grad_v], axis=1)
    grad_normed = dot(grad_kv, w_kv, ((1,), (1,)))
    grad_normed_own = grad_normed[:OWN] + dot(grad_q, w_q, ((1,), (1,)))

    def norm_back(values, inverse, grad):
        scaled = values * inverse
        gain_term = jnp.sum(grad * scaled, axis=0, keepdims=True)
        grad = grad * gain
        along = jnp.mean(grad * scaled, axis=-1, keepdims=True)
        return gain_term, inverse * (grad - scaled * along)

    start_plane(1)

    gain_own, image_own = norm_back(own_float, own_inverse, grad_normed_own)
    gain_halo, image_halo = norm_back(halo_float, halo_inverse, grad_normed[OWN:])
    gain_sum = gain_own + gain_halo
    grad_send[...] = image_halo.astype(BF16)
    for place, step in reversed(tuple(zip(PLACES, OWNERS))):
        there = pl.ds(place[0], place[1])
        remote(grad_send.at[there], grad_back.at[there], BACK_SEM, neighbour(step)).start()
    small_own[...] = jnp.concatenate(
        [scale_sum, gain_sum[:, :OWN], gain_sum[:, OWN:], jnp.zeros((5, OWN), F32)], axis=0
    )
    remote(small_own, small_core, SMALL_CORE, sibling).start()

    start_line(0)

    wait_received(small_core, SMALL_CORE)
    chip_small = small_own[...] + small_core[...]
    small_plane[chip] = chip_small

    @pl.when(chip != 0)
    def _():
        remote(
            small_plane.at[chip], small_plane.at[chip], SMALL_PLANE, (z * 2, core)
        ).start()

    mixed = attended_t.T.astype(BF16)
    output_ref[...] = (own_float + dot(mixed, w_out_ref[...])).astype(BF16)
    store(output_ref, output_hbm)

    start_line(1)

    @pl.when(chip == 0)
    def _():
        wait_received(small_plane.at[pl.ds(1, NP - 1)], SMALL_PLANE)
        plane = small_plane[0]
        for k in range(1, NP):
            plane = plane + small_plane[k]
        small_line[z] = plane

        @pl.when(z != 0)
        def _():
            remote(small_line.at[z], small_line.at[z], SMALL_LINE, z_id(0)).start()

    wait_received(grad_back, BACK_SEM)
    grad_image = cot.astype(F32) + image_own
    grad_image = grad_image + dot(sel, grad_back[pl.ds(96, 128), :], ((0,), (0,)))
    top = grad_back[pl.ds(48, 48), :].astype(F32)
    bottom = grad_back[pl.ds(0, 48), :].astype(F32)
    grad_image = jnp.concatenate(
        [grad_image[:48] + top, grad_image[48:80], grad_image[80:] + bottom], axis=0
    )
    grad_image_ref[...] = grad_image.astype(BF16)
    store(grad_image_ref, grad_image_hbm)

    start_gather(0)
    start_gather(1)

    @pl.when(chip == 0)
    def _():
        @pl.when(z == 0)
        def _():
            wait_received(small_line.at[pl.ds(1, NZ - 1)], SMALL_LINE)
            line = small_line[0]
            for k in range(1, NZ):
                line = line + small_line[k]
            small_total[...] = line * factor

        @pl.when(z != 0)
        def _():
            wait_received(small_total, SMALL_CAST)

        for other, device in peers:
            remote(small_total, small_total, SMALL_GATHER, device).start()

        @pl.when(z == 0)
        def _():
            for k in CAST_ORDER:
                remote(small_total, small_total, SMALL_CAST, z_id(k)).start()

    finish_gather(0)
    finish_gather(1)

    @pl.when(chip != 0)
    def _():
        wait_received(small_total, SMALL_GATHER)

    store(small_total, small_hbm)

    wait_received(gathered.at[1 - core], BOTH_SEM)
    grad_out_ref[...] = gathered[1].astype(F32)
    store(grad_out_ref, grad_out_hbm)
    grad_qkv_ref[:, pl.ds(2 * C, C)] = gathered[0].astype(F32)
    value_part = pl.ds(2 * C, C)
    store(grad_qkv_ref.at[:, value_part], grad_qkv_hbm.at[:, value_part])
    wait_received(gathered.at[3 - core], BOTH_SEM + 1)
    for j in range(2):
        part = pl.ds(j * C, C)
        grad_qkv_ref[:, part] = gathered[2 + j].astype(F32)
        store(grad_qkv_ref.at[:, part], grad_qkv_hbm.at[:, part])

    wait_sent(halo, HALO_SEM)
    wait_sent(grad_send, BACK_SEM)
    wait_sent(small_own, SMALL_CORE)
    for stage in range(2):
        wait_sent(core_send.at[stage], CORE_SEM + stage)
        wait_sent(plane_recv.at[stage], PLANE_SEM + stage)
        wait_sent(gathered.at[0, pl.ds(0, 240)], GATHER_SEM + stage)
        wait_sent(gathered.at[0], BOTH_SEM + stage)

    @pl.when(z != 0)
    def _():
        for stage in range(2):
            wait_sent(line_send.at[stage], LINE_SEM + stage)

    @pl.when(z == 0)
    def _():
        for stage in range(2):
            wait_sent(line_recv.at[stage, pl.ds(1, NZ - 1)], CAST_SEM + stage)

    @pl.when(chip != 0)
    def _():
        wait_sent(small_total, SMALL_PLANE)

    @pl.when(chip == 0)
    def _():
        wait_sent(small_plane.at[pl.ds(1, NP - 1)], SMALL_GATHER)

        @pl.when(z != 0)
        def _():
            wait_sent(small_total, SMALL_LINE)

        @pl.when(z == 0)
        def _():
            wait_sent(small_line.at[pl.ds(1, NZ - 1)], SMALL_CAST)

    for copy in stores:
        copy.wait()


def deliver(
    output,
    grad_image,
    grad_qkv,
    grad_out,
    small_ref,
    output_out,
    grad_image_out,
    grad_qkv_out,
    grad_out_out,
    gain_ref,
    scale_ref,
    qkv_ref,
    out_ref,
    output_ref,
    image_ref,
    sems,
):
    steps = (
        (grad_qkv, grad_qkv_out, qkv_ref),
        (grad_out, grad_out_out, out_ref),
        (output, output_out, output_ref),
        (grad_image, grad_image_out, image_ref),
    )
    loads = [pltpu.make_async_copy(a, c, sems.at[i]) for i, (a, b, c) in enumerate(steps)]
    copies = [pltpu.make_async_copy(c, b, sems.at[4 + i]) for i, (a, b, c) in enumerate(steps)]
    for load in loads:
        load.start()
    for load, copy in zip(loads, copies):
        load.wait()
        copy.start()
    gain_ref[:, pl.ds(0, OWN)] = small_ref[pl.ds(1, 1), :]
    gain_ref[:, pl.ds(OWN, OWN)] = small_ref[pl.ds(2, 1), :]
    scale_ref[...] = small_ref[pl.ds(0, 1), pl.ds(0, HEADS)]
    for copy in copies:
        copy.wait()


def on_device(image, w_qkv, w_out, norm_gain, head_scale, cotangent):
    rows = lax.axis_size("row")
    cols = lax.axis_size("col")
    vmem = pl.BlockSpec(memory_space=pltpu.VMEM)
    hbm = pl.BlockSpec(memory_space=pl.ANY)
    smem = pl.BlockSpec(memory_space=pltpu.SMEM)
    factor = 1.0 / math.sqrt(rows * TH * cols * TW)

    def kernel(*refs):
        block(rows, cols, factor, *refs)

    parts = pl.pallas_call(
        kernel,
        out_shape=(
            jax.ShapeDtypeStruct((OWN, C), BF16),
            jax.ShapeDtypeStruct((OWN, C), BF16),
            jax.ShapeDtypeStruct((C, 3 * C), F32),
            jax.ShapeDtypeStruct((C, C), F32),
            jax.ShapeDtypeStruct((8, OWN), F32),
        ),
        in_specs=[hbm, hbm, hbm, hbm, smem, hbm],
        out_specs=(hbm,) * 5,
        scratch_shapes=[
            pltpu.VMEM((OWN, C), BF16),
            pltpu.VMEM((C, 3 * C), BF16),
            pltpu.VMEM((C, C), BF16),
            pltpu.VMEM((1, C), F32),
            pltpu.VMEM((OWN, C), BF16),
            pltpu.VMEM((HALO, C), BF16),
            pltpu.VMEM((OWN, C), BF16),
            pltpu.VMEM((HALO, C), BF16),
            pltpu.VMEM((HALO, C), BF16),
            pltpu.VMEM((C, LANES), BF16),
            pltpu.VMEM((C, LANES), BF16),
            pltpu.VMEM((4, C, C), F32),
            pltpu.VMEM((2, C, C), BF16),
            pltpu.VMEM((2, C, C), BF16),
            pltpu.VMEM((2, C, C), F32),
            pltpu.VMEM((2, C, C), BF16),
            pltpu.VMEM((2, NP - 1, 16, C), BF16),
            pltpu.VMEM((2, 16, C), BF16),
            pltpu.VMEM((2, NZ, 16, C), BF16),
            pltpu.VMEM((4, C, C), BF16),
            pltpu.VMEM((8, OWN), F32),
            pltpu.VMEM((8, OWN), F32),
            pltpu.VMEM((NP, 8, OWN), F32),
            pltpu.VMEM((NZ, 8, OWN), F32),
            pltpu.VMEM((8, OWN), F32),
            pltpu.VMEM((OWN, C), BF16),
            pltpu.VMEM((OWN, C), BF16),
            pltpu.VMEM((C, 3 * C), F32),
            pltpu.VMEM((C, C), F32),
            pltpu.SemaphoreType.DMA((38,)),
            pltpu.SemaphoreType.DMA((12,)),
        ],
        compiler_params=pltpu.CompilerParams(
            collective_id=0, has_side_effects=True, vmem_limit_bytes=VMEM_LIMIT
        ),
    )(
        image.reshape(OWN, C),
        w_qkv,
        w_out,
        norm_gain.reshape(1, C),
        head_scale,
        cotangent.reshape(OWN, C),
    )
    output, grad_image, grad_qkv, grad_out, grad_gain, grad_scale = pl.pallas_call(
        deliver,
        out_shape=(
            jax.ShapeDtypeStruct((OWN, C), BF16),
            jax.ShapeDtypeStruct((OWN, C), BF16),
            jax.ShapeDtypeStruct((C, 3 * C), F32),
            jax.ShapeDtypeStruct((C, C), F32),
            jax.ShapeDtypeStruct((1, C), F32),
            jax.ShapeDtypeStruct((1, HEADS), F32),
        ),
        in_specs=[hbm, hbm, hbm, hbm, vmem],
        out_specs=(hbm, hbm, hbm, hbm, vmem, vmem),
        scratch_shapes=[
            pltpu.VMEM((C, 3 * C), F32),
            pltpu.VMEM((C, C), F32),
            pltpu.VMEM((OWN, C), BF16),
            pltpu.VMEM((OWN, C), BF16),
            pltpu.SemaphoreType.DMA((8,)),
        ],
        compiler_params=pltpu.CompilerParams(vmem_limit_bytes=VMEM_LIMIT),
    )(*parts)
    return (
        output.reshape(TH, TW, C),
        grad_image.reshape(TH, TW, C),
        grad_qkv,
        grad_out,
        grad_gain.reshape(C),
        grad_scale.reshape(HEADS),
    )


def solution(mesh):
    placed = (P("row", "col", None), P(), P(), P(), P(), P("row", "col", None))
    return jax.shard_map(
        on_device,
        mesh=mesh,
        in_specs=placed,
        out_specs=(P("row", "col", None), P("row", "col", None), P(), P(), P(), P()),
        check_vma=False,
    )
```

```python
import math

import jax
import jax.numpy as jnp
from jax import lax
from jax.experimental import pallas as pl
from jax.experimental.pallas import tpu as pltpu
from jax.sharding import PartitionSpec as P

C = 256
HEADS = 4
HEAD_DIM = 64
RADIUS = 3
TH = 8
TW = 16
OWN = TH * TW
HALO = 224
KEYS = OWN + HALO
LANES = HEADS * OWN
EPS = 1e-06
NP = 16
VMEM_LIMIT = 40 * 1024 * 1024
NZ = 16
MESH = pl.DeviceIdType.MESH
F32 = jnp.float32
BF16 = jnp.bfloat16

PLACES = (
    (0, 48, -3, 0, 16),
    (48, 48, TH, 0, 16),
    (96, 32, 0, -3, 4),
    (128, 32, 0, TW, 4),
    (160, 16, -3, -3, 4),
    (176, 16, -3, TW, 4),
    (192, 16, TH, -3, 4),
    (208, 16, TH, TW, 4),
)
OWNERS = ((-1, 0), (1, 0), (0, -1), (0, 1), (-1, -1), (-1, 1), (1, -1), (1, 1))

STEPS = sorted(
    ((dx, dy) for dx in range(4) for dy in range(4) if dx or dy),
    key=lambda step: (-min(step[0], 4 - step[0]) - min(step[1], 4 - step[1]), step),
)
CAST_ORDER = (1, 2, 3, 4, 5, 15, 6, 14, 7, 13, 8, 12, 9, 11, 10)
HALO_SEM, BACK_SEM, SMALL_CORE, SMALL_PLANE, SMALL_LINE, SMALL_CAST, SMALL_GATHER = range(7)
CORE_SEM, PLANE_SEM, LINE_SEM, CAST_SEM, GATHER_SEM, BOTH_SEM = range(7, 19, 2)


def dot(a, b, contract=((1,), (0,))):
    return lax.dot_general(a, b, (contract, ((), ())), preferred_element_type=F32)


def key_mask(row, col, height, breadth):
    blocks = []
    for first, count, y0, x0, across in ((-1, OWN, 0, 0, TW),) + PLACES:
        place = lax.broadcasted_iota(jnp.int32, (count, OWN), 0)
        query = lax.broadcasted_iota(jnp.int32, (count, OWN), 1)
        y = place // across + y0
        x = place % across + x0
        ok = (jnp.abs(y - query // TW) <= RADIUS) & (jnp.abs(x - query % TW) <= RADIUS)
        gy = y + row * TH
        gx = x + col * TW
        ok = ok & (gy >= 0) & (gy < height) & (gx >= 0) & (gx < breadth)
        if across == 4:
            ok = ok & (place % 4 < RADIUS)
            if count == 16:
                ok = ok & (place // 4 < RADIUS)
        blocks.append(jnp.where(ok, 1.0, 0.0).astype(F32))
    return jnp.concatenate(blocks, axis=0)


def selection():
    blocks = []
    for first, count, y0, x0, across in PLACES[2:]:
        place = lax.broadcasted_iota(jnp.int32, (count, OWN), 0)
        pixel = lax.broadcasted_iota(jnp.int32, (count, OWN), 1)
        y = place // 4 + (y0 + TH) % TH
        x = place % 4 + (x0 + TW) % TW
        ok = (pixel == y * TW + x) & (place % 4 < RADIUS)
        if count == 16:
            ok = ok & (place // 4 < RADIUS)
        blocks.append(jnp.where(ok, 1.0, 0.0).astype(F32))
    return jnp.concatenate(blocks, axis=0).astype(BF16)


def block(rows, cols, factor, *refs):
    (
        image_hbm,
        w_qkv_hbm,
        w_out_hbm,
        gain_hbm,
        scale_hbm,
        cot_hbm,
        output_ref,
        grad_image_ref,
        grad_qkv_ref,
        grad_out_ref,
        small_total,
        image_ref,
        w_qkv_ref,
        w_out_ref,
        gain_ref,
        scale_ref,
        cot_ref,
        halo,
        side,
        grad_send,
        grad_back,
        q_block,
        g_block,
        total,
        core_send,
        core_recv,
        mine,
        plane_send,
        plane_recv,
        line_send,
        line_recv,
        gathered,
        small_own,
        small_core,
        small_plane,
        small_line,
        sems,
        local_sems,
    ) = refs
    row = lax.axis_index("row")
    col = lax.axis_index("col")
    z = row // 2
    core = col % 2
    x = (col // 8) * 2 + row % 2
    y = (col // 2) % 4
    chip = x * 4 + y
    sibling = (row, col + 1 - 2 * core)

    loads = []
    for i, (src, dst) in enumerate(
        (
            (image_hbm, image_ref),
            (w_qkv_hbm, w_qkv_ref),
            (cot_hbm, cot_ref),
            (w_out_hbm, w_out_ref),
            (gain_hbm, gain_ref),
            (scale_hbm, scale_ref),
        )
    ):
        load = pltpu.make_async_copy(src, dst, local_sems.at[i])
        load.start()
        loads.append(load)

    def chip_id(ox, oy):
        return (z * 2 + ox % 2, (ox // 2) * 8 + oy * 2 + core)

    def z_id(other):
        return (other * 2 + row % 2, col)

    def neighbour(step):
        return (lax.rem(row + step[0] + rows, rows), lax.rem(col + step[1] + cols, cols))

    peers = []
    for dx, dy in STEPS:
        ox, oy = lax.rem(x + dx, 4), lax.rem(y + dy, 4)
        peers.append((ox * 4 + oy, chip_id(ox, oy)))

    barrier = pltpu.get_barrier_semaphore()

    def greet(device):
        pl.semaphore_signal(barrier, inc=1, device_id=device, device_id_type=MESH)

    for step in OWNERS:
        greet(neighbour(step))
    for other, device in peers:
        greet(device)

    @pl.when(z != 0)
    def _():
        greet(z_id(0))

    @pl.when(z == 0)
    def _():
        for k in range(1, NZ):
            greet(z_id(k))

    def remote(src, dst, sem, device):
        return pltpu.make_async_remote_copy(
            src_ref=src,
            dst_ref=dst,
            send_sem=sems.at[2 * sem],
            recv_sem=sems.at[2 * sem + 1],
            device_id=device,
            device_id_type=MESH,
        )

    def wait_sent(ref, sem):
        pltpu.make_async_copy(ref, ref, sems.at[2 * sem]).wait()

    def wait_received(ref, sem):
        pltpu.make_async_copy(ref, ref, sems.at[2 * sem + 1]).wait()

    sel = selection()
    loads[0].wait()
    side[...] = dot(sel, image_ref[...]).astype(BF16)

    @pl.when(z != 0)
    def _():
        pl.semaphore_wait(barrier, 8 + (NP - 1) + 1)

    @pl.when(z == 0)
    def _():
        pl.semaphore_wait(barrier, 8 + (NP - 1) + (NZ - 1))

    for place, step in reversed(tuple(zip(PLACES, OWNERS))):
        first, count = place[0], place[1]
        if first == 0:
            src = image_ref.at[pl.ds(OWN - 48, 48)]
        elif first == 48:
            src = image_ref.at[pl.ds(0, 48)]
        else:
            src = side.at[pl.ds(first - 96, count)]
        remote(
            src, halo.at[pl.ds(first, count)], HALO_SEM, neighbour((-step[0], -step[1]))
        ).start()

    for load in loads[1:]:
        load.wait()
    gain = gain_ref[...]
    w_q = w_qkv_ref[:, :C]
    w_kv = w_qkv_ref[:, C:]
    cot = cot_ref[...]
    mask = key_mask(row, col, rows * TH, cols * TW)

    def norm(values):
        inverse = lax.rsqrt(jnp.mean(values * values, axis=-1, keepdims=True) + EPS)
        return inverse, (values * inverse * gain).astype(BF16)

    own_float = image_ref[...].astype(F32)
    own_inverse, own_normed = norm(own_float)
    own_normed_t = own_normed.astype(F32).T.astype(BF16)
    query = dot(own_normed, w_q).astype(BF16)
    query_t = query.astype(F32).T
    q_block[...] = jnp.zeros_like(q_block)
    g_block[...] = jnp.zeros_like(g_block)
    grad_mixed_t = dot(w_out_ref[...], cot, ((1,), (1,)))
    q_inverse = []
    for h in range(HEADS):
        ch = slice(h * HEAD_DIM, (h + 1) * HEAD_DIM)
        ln = slice(h * OWN, (h + 1) * OWN)
        part = query_t[ch]
        q_block[ch, ln] = part.astype(BF16)
        g_block[ch, ln] = grad_mixed_t[ch].astype(BF16)
        q_inverse.append(lax.rsqrt(jnp.sum(part * part, axis=0, keepdims=True) + EPS))
    own_kv = dot(own_normed, w_kv)

    wait_received(halo, HALO_SEM)

    halo_float = halo[...].astype(F32)
    halo_inverse, halo_normed = norm(halo_float)
    halo_normed_t = halo_normed.astype(F32).T.astype(BF16)
    halo_kv = dot(halo_normed, w_kv)
    kv = jnp.concatenate([own_kv, halo_kv], axis=0).astype(BF16)
    keys = kv[:, :C]
    values = kv[:, C:]
    keys_float = keys.astype(F32)
    values_t = values.astype(F32).T.astype(BF16)
    normed_t = jnp.concatenate([own_normed_t, halo_normed_t], axis=1)

    scores = dot(keys, q_block[...])
    probs = []
    probs_bf = []
    logits = []
    k_inverse = []
    attended_t = []
    for h in range(HEADS):
        ch = slice(h * HEAD_DIM, (h + 1) * HEAD_DIM)
        ln = slice(h * OWN, (h + 1) * OWN)
        k_part = keys_float[:, ch]
        k_inv = lax.rsqrt(jnp.sum(k_part * k_part, axis=1, keepdims=True) + EPS)
        logit = scores[:, ln] * k_inv * (q_inverse[h] * scale_ref[0, h])
        weight = jnp.exp(logit) * mask
        prob = weight * (1.0 / jnp.sum(weight, axis=0, keepdims=True))
        probs.append(prob)
        probs_bf.append(prob.astype(BF16))
        logits.append(logit)
        k_inverse.append(k_inv)
        attended_t.append(dot(values_t[ch], probs_bf[h]))
    attended_t = jnp.concatenate(attended_t, axis=0)
    grad_v = dot(jnp.concatenate(probs_bf, axis=1), g_block[...], ((1,), (1,))).astype(BF16)

    def start_core(stage):
        core_send[stage] = total[2 * stage + 1 - core].astype(BF16)
        remote(core_send.at[stage], core_recv.at[stage], CORE_SEM + stage, sibling).start()

    def start_plane(stage):
        wait_received(core_recv.at[stage], CORE_SEM + stage)
        summed = total[2 * stage + core] + core_recv[stage].astype(F32)
        mine[stage] = summed
        plane_send[stage] = summed.astype(BF16)
        for k, (other, device) in enumerate(peers):
            remote(
                plane_send.at[stage, pl.ds(pl.multiple_of(other * 16, 16), 16)],
                plane_recv.at[stage, k],
                PLANE_SEM + stage,
                device,
            ).start()

    def start_line(stage):
        fifteen = plane_recv.at[stage]
        wait_received(fifteen, PLANE_SEM + stage)
        summed = mine[stage, pl.ds(pl.multiple_of(chip * 16, 16), 16), :]
        for k in range(NP - 1):
            summed = summed + plane_recv[stage, k].astype(F32)

        @pl.when(z != 0)
        def _():
            line_send[stage] = summed.astype(BF16)
            remote(
                line_send.at[stage], line_recv.at[stage, z], LINE_SEM + stage, z_id(0)
            ).start()

        @pl.when(z == 0)
        def _():
            mine[stage, pl.ds(0, 16), :] = summed

    here = pl.ds(pl.multiple_of(chip * 16, 16), 16)

    def spot(stage):
        return gathered.at[2 * stage + core, here]

    def start_gather(stage):
        @pl.when(z == 0)
        def _():
            wait_received(line_recv.at[stage, pl.ds(1, NZ - 1)], LINE_SEM + stage)
            summed = mine[stage, pl.ds(0, 16), :]
            for k in range(1, NZ):
                summed = summed + line_recv[stage, k].astype(F32)
            gathered[2 * stage + core, here, :] = (summed * factor).astype(BF16)

        @pl.when(z != 0)
        def _():
            wait_received(spot(stage), CAST_SEM + stage)

        @pl.when(z == 0)
        def _():
            for k in CAST_ORDER[:4]:
                remote(spot(stage), spot(stage), CAST_SEM + stage, z_id(k)).start()

        for other, device in peers:
            remote(spot(stage), spot(stage), GATHER_SEM + stage, device).start()

        @pl.when(z == 0)
        def _():
            for k in CAST_ORDER[4:]:
                remote(spot(stage), spot(stage), CAST_SEM + stage, z_id(k)).start()

    def finish_gather(stage):
        own = gathered.at[2 * stage + core]
        wait_received(own.at[pl.ds(0, 240)], GATHER_SEM + stage)
        remote(own, own, BOTH_SEM + stage, sibling).start()

    mixed_t = attended_t.astype(BF16)
    total[0] = dot(normed_t, grad_v)
    total[1] = dot(mixed_t, cot)
    start_core(0)

    grad_probs = dot(values, g_block[...])
    keys_t = keys_float.T.astype(BF16)
    grad_logits = []
    k_along = []
    grad_q_t = []
    scale_sum = jnp.zeros((1, OWN), F32)
    lane = lax.broadcasted_iota(jnp.int32, (1, OWN), 1)
    for h in range(HEADS):
        ch = slice(h * HEAD_DIM, (h + 1) * HEAD_DIM)
        ln = slice(h * OWN, (h + 1) * OWN)
        scale = scale_ref[0, h]
        prob = probs[h]
        grad_prob = grad_probs[:, ln]
        row_dot = jnp.sum(prob * grad_prob, axis=0, keepdims=True)
        grad_logit = prob * (grad_prob - row_dot)
        product = grad_logit * logits[h]
        along_q = jnp.sum(product, axis=0, keepdims=True)
        scale_sum = scale_sum + jnp.where(
            lane == h, jnp.sum(along_q, axis=1, keepdims=True) / scale, 0.0
        )
        k_along.append(jnp.sum(product, axis=1, keepdims=True))
        grad_logits.append((grad_logit * (q_inverse[h] * scale)).astype(BF16))
        unit_grad = dot(keys_t[ch], (grad_logit * (k_inverse[h] * scale)).astype(BF16))
        grad_q_t.append(
            q_inverse[h] * (unit_grad - query_t[ch] * (q_inverse[h] * along_q))
        )

    grad_q = jnp.concatenate(grad_q_t, axis=0).T.astype(BF16)
    grad_k_unit = dot(jnp.concatenate(grad_logits, axis=1), q_block[...], ((1,), (1,)))
    low = lax.broadcasted_iota(jnp.int32, (1, OWN), 1) < HEAD_DIM
    grad_k = []
    for t in range(2):
        ln = slice(t * OWN, (t + 1) * OWN)
        inv = jnp.where(low, k_inverse[2 * t], k_inverse[2 * t + 1])
        along = jnp.where(low, k_along[2 * t], k_along[2 * t + 1])
        grad_k.append(inv * (grad_k_unit[:, ln] - keys_float[:, ln] * (inv * along)))
    grad_k = jnp.concatenate(grad_k, axis=1).astype(BF16)

    total[2] = dot(own_normed_t, grad_q)
    total[3] = dot(normed_t, grad_k)
    start_core(1)
    start_plane(0)

    grad_kv = jnp.concatenate([grad_k, grad_v], axis=1)
    grad_normed = dot(grad_kv, w_kv, ((1,), (1,)))
    grad_normed_own = grad_normed[:OWN] + dot(grad_q, w_q, ((1,), (1,)))

    def norm_back(values, inverse, grad):
        scaled = values * inverse
        gain_term = jnp.sum(grad * scaled, axis=0, keepdims=True)
        grad = grad * gain
        along = jnp.mean(grad * scaled, axis=-1, keepdims=True)
        return gain_term, inverse * (grad - scaled * along)

    start_plane(1)

    gain_own, image_own = norm_back(own_float, own_inverse, grad_normed_own)
    gain_halo, image_halo = norm_back(halo_float, halo_inverse, grad_normed[OWN:])
    gain_sum = gain_own + gain_halo
    grad_send[...] = image_halo.astype(BF16)
    for place, step in reversed(tuple(zip(PLACES, OWNERS))):
        there = pl.ds(place[0], place[1])
        remote(grad_send.at[there], grad_back.at[there], BACK_SEM, neighbour(step)).start()
    small_own[...] = jnp.concatenate(
        [scale_sum, gain_sum[:, :OWN], gain_sum[:, OWN:], jnp.zeros((5, OWN), F32)], axis=0
    )
    remote(small_own, small_core, SMALL_CORE, sibling).start()

    start_line(0)

    wait_received(small_core, SMALL_CORE)
    chip_small = small_own[...] + small_core[...]
    small_plane[chip] = chip_small

    @pl.when(chip != 0)
    def _():
        remote(
            small_plane.at[chip], small_plane.at[chip], SMALL_PLANE, (z * 2, core)
        ).start()

    mixed = attended_t.T.astype(BF16)
    output_ref[...] = (own_float + dot(mixed, w_out_ref[...])).astype(BF16)

    start_line(1)

    @pl.when(chip == 0)
    def _():
        wait_received(small_plane.at[pl.ds(1, NP - 1)], SMALL_PLANE)
        plane = small_plane[0]
        for k in range(1, NP):
            plane = plane + small_plane[k]
        small_line[z] = plane

        @pl.when(z != 0)
        def _():
            remote(small_line.at[z], small_line.at[z], SMALL_LINE, z_id(0)).start()

    wait_received(grad_back, BACK_SEM)
    grad_image = cot.astype(F32) + image_own
    grad_image = grad_image + dot(sel, grad_back[pl.ds(96, 128), :], ((0,), (0,)))
    top = grad_back[pl.ds(48, 48), :].astype(F32)
    bottom = grad_back[pl.ds(0, 48), :].astype(F32)
    grad_image = jnp.concatenate(
        [grad_image[:48] + top, grad_image[48:80], grad_image[80:] + bottom], axis=0
    )
    grad_image_ref[...] = grad_image.astype(BF16)

    start_gather(0)
    start_gather(1)

    @pl.when(chip == 0)
    def _():
        @pl.when(z == 0)
        def _():
            wait_received(small_line.at[pl.ds(1, NZ - 1)], SMALL_LINE)
            line = small_line[0]
            for k in range(1, NZ):
                line = line + small_line[k]
            small_total[...] = line * factor

        @pl.when(z != 0)
        def _():
            wait_received(small_total, SMALL_CAST)

        for other, device in peers:
            remote(small_total, small_total, SMALL_GATHER, device).start()

        @pl.when(z == 0)
        def _():
            for k in CAST_ORDER:
                remote(small_total, small_total, SMALL_CAST, z_id(k)).start()

    finish_gather(0)
    finish_gather(1)

    @pl.when(chip != 0)
    def _():
        wait_received(small_total, SMALL_GATHER)


    wait_received(gathered.at[1 - core], BOTH_SEM)
    grad_out_ref[...] = gathered[1].astype(F32)
    grad_qkv_ref[:, pl.ds(2 * C, C)] = gathered[0].astype(F32)
    wait_received(gathered.at[3 - core], BOTH_SEM + 1)
    for j in range(2):
        part = pl.ds(j * C, C)
        grad_qkv_ref[:, part] = gathered[2 + j].astype(F32)

    wait_sent(halo, HALO_SEM)
    wait_sent(grad_send, BACK_SEM)
    wait_sent(small_own, SMALL_CORE)
    for stage in range(2):
        wait_sent(core_send.at[stage], CORE_SEM + stage)
        wait_sent(plane_recv.at[stage], PLANE_SEM + stage)
        wait_sent(gathered.at[0, pl.ds(0, 240)], GATHER_SEM + stage)
        wait_sent(gathered.at[0], BOTH_SEM + stage)

    @pl.when(z != 0)
    def _():
        for stage in range(2):
            wait_sent(line_send.at[stage], LINE_SEM + stage)

    @pl.when(z == 0)
    def _():
        for stage in range(2):
            wait_sent(line_recv.at[stage, pl.ds(1, NZ - 1)], CAST_SEM + stage)

    @pl.when(chip != 0)
    def _():
        wait_sent(small_total, SMALL_PLANE)

    @pl.when(chip == 0)
    def _():
        wait_sent(small_plane.at[pl.ds(1, NP - 1)], SMALL_GATHER)

        @pl.when(z != 0)
        def _():
            wait_sent(small_total, SMALL_LINE)

        @pl.when(z == 0)
        def _():
            wait_sent(small_line.at[pl.ds(1, NZ - 1)], SMALL_CAST)


def deliver(
    output,
    grad_image,
    grad_qkv,
    grad_out,
    small,
    output_out,
    grad_image_out,
    grad_qkv_out,
    grad_out_out,
    gain_out,
    scale_out,
    gain_ref,
    scale_ref,
    sems,
):
    steps = (
        (grad_qkv, grad_qkv_out),
        (grad_out, grad_out_out),
        (output, output_out),
        (grad_image, grad_image_out),
        (gain_ref, gain_out),
        (scale_ref, scale_out),
    )
    copies = [pltpu.make_async_copy(a, b, sems.at[i]) for i, (a, b) in enumerate(steps)]
    for copy in copies[:4]:
        copy.start()
    gain_ref[:, pl.ds(0, OWN)] = small[pl.ds(1, 1), :]
    gain_ref[:, pl.ds(OWN, OWN)] = small[pl.ds(2, 1), :]
    scale_ref[...] = small[pl.ds(0, 1), pl.ds(0, HEADS)]
    for copy in copies[4:]:
        copy.start()
    for copy in copies:
        copy.wait()


def on_device(image, w_qkv, w_out, norm_gain, head_scale, cotangent):
    rows = lax.axis_size("row")
    cols = lax.axis_size("col")
    vmem = pl.BlockSpec(memory_space=pltpu.VMEM)
    hbm = pl.BlockSpec(memory_space=pl.ANY)
    factor = 1.0 / math.sqrt(rows * TH * cols * TW)

    def kernel(*refs):
        block(rows, cols, factor, *refs)

    def pinned(array):
        return pltpu.with_memory_space_constraint(array, pltpu.HBM)

    parts = pl.pallas_call(
        kernel,
        out_shape=(
            pltpu.VMEM((OWN, C), BF16),
            pltpu.VMEM((OWN, C), BF16),
            pltpu.VMEM((C, 3 * C), F32),
            pltpu.VMEM((C, C), F32),
            pltpu.VMEM((8, OWN), F32),
        ),
        in_specs=[hbm] * 6,
        out_specs=(vmem,) * 5,
        scratch_shapes=[
            pltpu.VMEM((OWN, C), BF16),
            pltpu.VMEM((C, 3 * C), BF16),
            pltpu.VMEM((C, C), BF16),
            pltpu.VMEM((1, C), F32),
            pltpu.SMEM((1, HEADS), F32),
            pltpu.VMEM((OWN, C), BF16),
            pltpu.VMEM((HALO, C), BF16),
            pltpu.VMEM((OWN, C), BF16),
            pltpu.VMEM((HALO, C), BF16),
            pltpu.VMEM((HALO, C), BF16),
            pltpu.VMEM((C, LANES), BF16),
            pltpu.VMEM((C, LANES), BF16),
            pltpu.VMEM((4, C, C), F32),
            pltpu.VMEM((2, C, C), BF16),
            pltpu.VMEM((2, C, C), BF16),
            pltpu.VMEM((2, C, C), F32),
            pltpu.VMEM((2, C, C), BF16),
            pltpu.VMEM((2, NP - 1, 16, C), BF16),
            pltpu.VMEM((2, 16, C), BF16),
            pltpu.VMEM((2, NZ, 16, C), BF16),
            pltpu.VMEM((4, C, C), BF16),
            pltpu.VMEM((8, OWN), F32),
            pltpu.VMEM((8, OWN), F32),
            pltpu.VMEM((NP, 8, OWN), F32),
            pltpu.VMEM((NZ, 8, OWN), F32),
            pltpu.SemaphoreType.DMA((38,)),
            pltpu.SemaphoreType.DMA((6,)),
        ],
        compiler_params=pltpu.CompilerParams(
            collective_id=0, has_side_effects=True, vmem_limit_bytes=VMEM_LIMIT
        ),
    )(
        *map(
            pinned,
            (
                image.reshape(OWN, C),
                w_qkv,
                w_out,
                norm_gain.reshape(1, C),
                head_scale.reshape(1, HEADS),
                cotangent.reshape(OWN, C),
            ),
        )
    )
    output, grad_image, grad_qkv, grad_out, grad_gain, grad_scale = pl.pallas_call(
        deliver,
        out_shape=(
            jax.ShapeDtypeStruct((OWN, C), BF16),
            jax.ShapeDtypeStruct((OWN, C), BF16),
            jax.ShapeDtypeStruct((C, 3 * C), F32),
            jax.ShapeDtypeStruct((C, C), F32),
            jax.ShapeDtypeStruct((1, C), F32),
            jax.ShapeDtypeStruct((1, HEADS), F32),
        ),
        in_specs=[vmem] * 5,
        out_specs=(hbm,) * 6,
        scratch_shapes=[
            pltpu.VMEM((1, C), F32),
            pltpu.VMEM((1, HEADS), F32),
            pltpu.SemaphoreType.DMA((6,)),
        ],
        compiler_params=pltpu.CompilerParams(vmem_limit_bytes=VMEM_LIMIT),
    )(*(pltpu.with_memory_space_constraint(part, pltpu.VMEM) for part in parts))
    return (
        output.reshape(TH, TW, C),
        grad_image.reshape(TH, TW, C),
        grad_qkv,
        grad_out,
        grad_gain.reshape(C),
        grad_scale.reshape(HEADS),
    )


def solution(mesh):
    placed = (P("row", "col", None), P(), P(), P(), P(), P("row", "col", None))
    return jax.shard_map(
        on_device,
        mesh=mesh,
        in_specs=placed,
        out_specs=(P("row", "col", None), P("row", "col", None), P(), P(), P(), P()),
        check_vma=False,
    )
```

```python
import math

import jax
import jax.numpy as jnp
from jax import lax
from jax.experimental import pallas as pl
from jax.experimental.pallas import tpu as pltpu
from jax.sharding import PartitionSpec as P

C = 256
HEADS = 4
HEAD_DIM = 64
RADIUS = 3
TH = 8
TW = 16
OWN = TH * TW
HALO = 224
KEYS = OWN + HALO
LANES = HEADS * OWN
EPS = 1e-06
NP = 16
VMEM_LIMIT = 40 * 1024 * 1024
NZ = 16
MESH = pl.DeviceIdType.MESH
F32 = jnp.float32
BF16 = jnp.bfloat16

PLACES = (
    (0, 48, -3, 0, 16),
    (48, 48, TH, 0, 16),
    (96, 32, 0, -3, 4),
    (128, 32, 0, TW, 4),
    (160, 16, -3, -3, 4),
    (176, 16, -3, TW, 4),
    (192, 16, TH, -3, 4),
    (208, 16, TH, TW, 4),
)
OWNERS = ((-1, 0), (1, 0), (0, -1), (0, 1), (-1, -1), (-1, 1), (1, -1), (1, 1))

STEPS = sorted(
    ((dx, dy) for dx in range(4) for dy in range(4) if dx or dy),
    key=lambda step: (-min(step[0], 4 - step[0]) - min(step[1], 4 - step[1]), step),
)
OWNER_PLANES = 2
CASTS = ((10, 11, 12, 13, 14, 15), (2, 3, 4, 5, 6, 7, 8, 9))
CASTS_FIRST = (2, 4)
HALO_SEM, BACK_SEM, SMALL_CORE, SMALL_PLANE, SMALL_LINE, SMALL_CAST, SMALL_GATHER = range(7)
CAST_SEM, GATHER_SEM, BOTH_SEM = range(7, 10)
CORE_SEM, PLANE_SEM, LINE_SEM = range(10, 16, 2)


def dot(a, b, contract=((1,), (0,))):
    return lax.dot_general(a, b, (contract, ((), ())), preferred_element_type=F32)


def key_mask(row, col, height, breadth):
    blocks = []
    for first, count, y0, x0, across in ((-1, OWN, 0, 0, TW),) + PLACES:
        place = lax.broadcasted_iota(jnp.int32, (count, OWN), 0)
        query = lax.broadcasted_iota(jnp.int32, (count, OWN), 1)
        y = place // across + y0
        x = place % across + x0
        ok = (jnp.abs(y - query // TW) <= RADIUS) & (jnp.abs(x - query % TW) <= RADIUS)
        gy = y + row * TH
        gx = x + col * TW
        ok = ok & (gy >= 0) & (gy < height) & (gx >= 0) & (gx < breadth)
        if across == 4:
            ok = ok & (place % 4 < RADIUS)
            if count == 16:
                ok = ok & (place // 4 < RADIUS)
        blocks.append(jnp.where(ok, 1.0, 0.0).astype(F32))
    return jnp.concatenate(blocks, axis=0)


def selection():
    blocks = []
    for first, count, y0, x0, across in PLACES[2:]:
        place = lax.broadcasted_iota(jnp.int32, (count, OWN), 0)
        pixel = lax.broadcasted_iota(jnp.int32, (count, OWN), 1)
        y = place // 4 + (y0 + TH) % TH
        x = place % 4 + (x0 + TW) % TW
        ok = (pixel == y * TW + x) & (place % 4 < RADIUS)
        if count == 16:
            ok = ok & (place // 4 < RADIUS)
        blocks.append(jnp.where(ok, 1.0, 0.0).astype(F32))
    return jnp.concatenate(blocks, axis=0).astype(BF16)


def block(rows, cols, factor, *refs):
    (
        image_hbm,
        w_qkv_hbm,
        w_out_hbm,
        gain_hbm,
        scale_hbm,
        cot_hbm,
        output_ref,
        grad_image_ref,
        grad_qkv_ref,
        grad_out_ref,
        small_total,
        image_ref,
        w_qkv_ref,
        w_out_ref,
        gain_ref,
        scale_ref,
        cot_ref,
        halo,
        side,
        grad_send,
        grad_back,
        q_block,
        g_block,
        total,
        core_send,
        core_recv,
        mine,
        plane_send,
        plane_recv,
        line_send,
        line_recv,
        gathered,
        small_own,
        small_core,
        small_plane,
        small_line,
        sems,
        local_sems,
    ) = refs
    row = lax.axis_index("row")
    col = lax.axis_index("col")
    z = row // 2
    core = col % 2
    x = (col // 8) * 2 + row % 2
    y = (col // 2) % 4
    chip = x * 4 + y
    sibling = (row, col + 1 - 2 * core)

    loads = []
    for i, (src, dst) in enumerate(
        (
            (image_hbm, image_ref),
            (w_qkv_hbm, w_qkv_ref),
            (cot_hbm, cot_ref),
            (w_out_hbm, w_out_ref),
            (gain_hbm, gain_ref),
            (scale_hbm, scale_ref),
        )
    ):
        load = pltpu.make_async_copy(src, dst, local_sems.at[i])
        load.start()
        loads.append(load)

    def chip_id(ox, oy):
        return (z * 2 + ox % 2, (ox // 2) * 8 + oy * 2 + core)

    def z_id(other):
        return (other * 2 + row % 2, col)

    def neighbour(step):
        return (lax.rem(row + step[0] + rows, rows), lax.rem(col + step[1] + cols, cols))

    peers = []
    for dx, dy in STEPS:
        ox, oy = lax.rem(x + dx, 4), lax.rem(y + dy, 4)
        peers.append((ox * 4 + oy, chip_id(ox, oy)))

    barrier = pltpu.get_barrier_semaphore()

    def greet(device):
        pl.semaphore_signal(barrier, inc=1, device_id=device, device_id_type=MESH)

    for step in OWNERS:
        greet(neighbour(step))
    for other, device in peers:
        greet(device)

    @pl.when(z < OWNER_PLANES)
    def _():
        for k in range(1, NZ):
            greet(z_id(lax.rem(z + k, NZ)))

    @pl.when(z >= OWNER_PLANES)
    def _():
        greet(z_id(jnp.where(z >= 10, 0, 1)))

    def remote(src, dst, sem, device):
        return pltpu.make_async_remote_copy(
            src_ref=src,
            dst_ref=dst,
            send_sem=sems.at[2 * sem],
            recv_sem=sems.at[2 * sem + 1],
            device_id=device,
            device_id_type=MESH,
        )

    def wait_sent(ref, sem):
        pltpu.make_async_copy(ref, ref, sems.at[2 * sem]).wait()

    def wait_received(ref, sem):
        pltpu.make_async_copy(ref, ref, sems.at[2 * sem + 1]).wait()

    sel = selection()
    loads[0].wait()
    side[...] = dot(sel, image_ref[...]).astype(BF16)

    @pl.when(z >= OWNER_PLANES)
    def _():
        pl.semaphore_wait(barrier, 8 + (NP - 1) + OWNER_PLANES)

    for owner in range(OWNER_PLANES):

        @pl.when(z == owner)
        def _():
            pl.semaphore_wait(barrier, 8 + (NP - 1) + 1 + len(CASTS[owner]))

    for place, step in reversed(tuple(zip(PLACES, OWNERS))):
        first, count = place[0], place[1]
        if first == 0:
            src = image_ref.at[pl.ds(OWN - 48, 48)]
        elif first == 48:
            src = image_ref.at[pl.ds(0, 48)]
        else:
            src = side.at[pl.ds(first - 96, count)]
        remote(
            src, halo.at[pl.ds(first, count)], HALO_SEM, neighbour((-step[0], -step[1]))
        ).start()

    for load in loads[1:]:
        load.wait()
    gain = gain_ref[...]
    w_q = w_qkv_ref[:, :C]
    w_kv = w_qkv_ref[:, C:]
    cot = cot_ref[...]
    mask = key_mask(row, col, rows * TH, cols * TW)

    def norm(values):
        inverse = lax.rsqrt(jnp.mean(values * values, axis=-1, keepdims=True) + EPS)
        return inverse, (values * inverse * gain).astype(BF16)

    own_float = image_ref[...].astype(F32)
    own_inverse, own_normed = norm(own_float)
    own_normed_t = own_normed.astype(F32).T.astype(BF16)
    query = dot(own_normed, w_q).astype(BF16)
    query_t = query.astype(F32).T
    q_block[...] = jnp.zeros_like(q_block)
    g_block[...] = jnp.zeros_like(g_block)
    grad_mixed_t = dot(w_out_ref[...], cot, ((1,), (1,)))
    q_inverse = []
    for h in range(HEADS):
        ch = slice(h * HEAD_DIM, (h + 1) * HEAD_DIM)
        ln = slice(h * OWN, (h + 1) * OWN)
        part = query_t[ch]
        q_block[ch, ln] = part.astype(BF16)
        g_block[ch, ln] = grad_mixed_t[ch].astype(BF16)
        q_inverse.append(lax.rsqrt(jnp.sum(part * part, axis=0, keepdims=True) + EPS))

    def segment(normed, mask_part):
        kv = dot(normed, w_kv).astype(BF16)
        keys = kv[:, :C]
        values = kv[:, C:]
        keys_float = keys.astype(F32)
        scores = dot(keys, q_block[...])
        weights = []
        logits = []
        inverses = []
        for h in range(HEADS):
            k_part = keys_float[:, h * HEAD_DIM : (h + 1) * HEAD_DIM]
            inverse = lax.rsqrt(jnp.sum(k_part * k_part, axis=1, keepdims=True) + EPS)
            logit = scores[:, h * OWN : (h + 1) * OWN] * inverse
            logit = logit * (q_inverse[h] * scale_ref[0, h])
            weights.append(jnp.exp(logit) * mask_part)
            logits.append(logit)
            inverses.append(inverse)
        keys_t = keys_float.T.astype(BF16)
        values_t = values.astype(F32).T.astype(BF16)
        grad_probs = dot(values, g_block[...])
        return keys_float, keys_t, values_t, weights, logits, inverses, grad_probs

    own_part = segment(own_normed, mask[:OWN])

    wait_received(halo, HALO_SEM)

    halo_float = halo[...].astype(F32)
    halo_inverse, halo_normed = norm(halo_float)
    halo_normed_t = halo_normed.astype(F32).T.astype(BF16)
    parts = (own_part, segment(halo_normed, mask[OWN:]))
    normed_t = (own_normed_t, halo_normed_t)
    probs = ([], [])
    probs_bf = ([], [])
    attended_t = []
    for h in range(HEADS):
        ch = slice(h * HEAD_DIM, (h + 1) * HEAD_DIM)
        weights = [part[3][h] for part in parts]
        weight_sum = sum(jnp.sum(weight, axis=0, keepdims=True) for weight in weights)
        inverse_sum = 1.0 / weight_sum
        mixed_head = 0.0
        for i in range(2):
            prob = weights[i] * inverse_sum
            probs[i].append(prob)
            probs_bf[i].append(prob.astype(BF16))
            mixed_head = mixed_head + dot(parts[i][2][ch], probs_bf[i][h])
        attended_t.append(mixed_head)
    attended_t = jnp.concatenate(attended_t, axis=0)
    grad_v = [
        dot(jnp.concatenate(probs_bf[i], axis=1), g_block[...], ((1,), (1,))).astype(BF16)
        for i in range(2)
    ]

    def start_core(stage):
        core_send[stage] = total[2 * stage + 1 - core].astype(BF16)
        remote(core_send.at[stage], core_recv.at[stage], CORE_SEM + stage, sibling).start()

    def start_plane(stage):
        wait_received(core_recv.at[stage], CORE_SEM + stage)
        summed = total[2 * stage + core] + core_recv[stage].astype(F32)
        mine[stage] = summed
        plane_send[stage] = summed.astype(BF16)
        for k, (other, device) in enumerate(peers):
            remote(
                plane_send.at[stage, pl.ds(pl.multiple_of(other * 16, 16), 16)],
                plane_recv.at[stage, k],
                PLANE_SEM + stage,
                device,
            ).start()

    def start_line(stage):
        fifteen = plane_recv.at[stage]
        wait_received(fifteen, PLANE_SEM + stage)
        summed = mine[stage, pl.ds(pl.multiple_of(chip * 16, 16), 16), :]
        for k in range(NP - 1):
            summed = summed + plane_recv[stage, k].astype(F32)

        summed = summed.astype(BF16)

        line_send[stage] = summed
        slot = line_recv.at[stage, z]

        @pl.when(z >= OWNER_PLANES)
        def _():
            for k in range(OWNER_PLANES):
                remote(line_send.at[stage], slot, LINE_SEM + stage, z_id(k)).start()

        @pl.when(z < OWNER_PLANES)
        def _():
            line_recv[stage, z] = summed
            remote(line_send.at[stage], slot, LINE_SEM + stage, z_id(1 - z)).start()

    def cast(ref, sem, ahead):
        for owner in range(OWNER_PLANES):

            @pl.when(z == owner)
            def _():
                first = CASTS_FIRST[owner]
                for k in CASTS[owner][:first] if ahead else CASTS[owner][first:]:
                    remote(ref, ref, sem, z_id(k)).start()

    spot = gathered.at[core, chip]
    own_half = gathered.at[core]

    def start_gather():
        @pl.when(z < OWNER_PLANES)
        def _():
            for stage in range(2):
                wait_received(line_recv.at[stage, pl.ds(0, NZ - 1)], LINE_SEM + stage)
                summed = line_recv[stage, 0].astype(F32)
                for k in range(1, NZ):
                    summed = summed + line_recv[stage, k].astype(F32)
                gathered[core, chip, stage] = (summed * factor).astype(BF16)

        cast(spot, CAST_SEM, True)

        @pl.when(z >= OWNER_PLANES)
        def _():
            wait_received(spot, CAST_SEM)

        for other, device in peers:
            remote(spot, spot, GATHER_SEM, device).start()

    def deliver_half(side):
        values = [gathered[side, :, stage].reshape(C, C).astype(F32) for stage in range(2)]
        if side == 0:
            grad_qkv_ref[:, pl.ds(2 * C, C)] = values[0]
            grad_qkv_ref[:, pl.ds(0, C)] = values[1]
        else:
            grad_out_ref[...] = values[0]
            grad_qkv_ref[:, pl.ds(C, C)] = values[1]

    mixed_t = attended_t.astype(BF16)
    total[0] = dot(normed_t[0], grad_v[0]) + dot(normed_t[1], grad_v[1])
    total[1] = dot(mixed_t, cot)
    start_core(0)

    grad_logits = ([], [])
    k_along = ([], [])
    grad_q_t = []
    scale_sum = jnp.zeros((1, OWN), F32)
    lane = lax.broadcasted_iota(jnp.int32, (1, OWN), 1)
    for h in range(HEADS):
        ch = slice(h * HEAD_DIM, (h + 1) * HEAD_DIM)
        ln = slice(h * OWN, (h + 1) * OWN)
        scale = scale_ref[0, h]
        grad_probs = [part[6][:, ln] for part in parts]
        row_dot = sum(
            jnp.sum(probs[i][h] * grad_probs[i], axis=0, keepdims=True) for i in range(2)
        )
        along_q = 0.0
        unit_grad = 0.0
        for i in range(2):
            grad_logit = probs[i][h] * (grad_probs[i] - row_dot)
            product = grad_logit * parts[i][4][h]
            along_q = along_q + jnp.sum(product, axis=0, keepdims=True)
            k_along[i].append(jnp.sum(product, axis=1, keepdims=True))
            grad_logits[i].append((grad_logit * (q_inverse[h] * scale)).astype(BF16))
            unit_grad = unit_grad + dot(
                parts[i][1][ch], (grad_logit * (parts[i][5][h] * scale)).astype(BF16)
            )
        scale_sum = scale_sum + jnp.where(
            lane == h, jnp.sum(along_q, axis=1, keepdims=True) / scale, 0.0
        )
        grad_q_t.append(
            q_inverse[h] * (unit_grad - query_t[ch] * (q_inverse[h] * along_q))
        )

    start_plane(0)
    grad_q = jnp.concatenate(grad_q_t, axis=0).T.astype(BF16)
    low = lax.broadcasted_iota(jnp.int32, (1, OWN), 1) < HEAD_DIM
    grad_k = []
    for i in range(2):
        unit_grad = dot(jnp.concatenate(grad_logits[i], axis=1), q_block[...], ((1,), (1,)))
        keys_float, inverses = parts[i][0], parts[i][5]
        pieces = []
        for t in range(2):
            ln = slice(t * OWN, (t + 1) * OWN)
            inv = jnp.where(low, inverses[2 * t], inverses[2 * t + 1])
            along = jnp.where(low, k_along[i][2 * t], k_along[i][2 * t + 1])
            pieces.append(inv * (unit_grad[:, ln] - keys_float[:, ln] * (inv * along)))
        grad_k.append(jnp.concatenate(pieces, axis=1).astype(BF16))

    total[2] = dot(own_normed_t, grad_q)
    total[3] = dot(normed_t[0], grad_k[0]) + dot(normed_t[1], grad_k[1])
    start_core(1)

    grad_normed = [
        dot(jnp.concatenate([grad_k[i], grad_v[i]], axis=1), w_kv, ((1,), (1,)))
        for i in range(2)
    ]
    grad_normed[0] = grad_normed[0] + dot(grad_q, w_q, ((1,), (1,)))

    def norm_back(values, inverse, grad):
        scaled = values * inverse
        gain_term = jnp.sum(grad * scaled, axis=0, keepdims=True)
        grad = grad * gain
        along = jnp.mean(grad * scaled, axis=-1, keepdims=True)
        return gain_term, inverse * (grad - scaled * along)

    gain_own, image_own = norm_back(own_float, own_inverse, grad_normed[0])
    gain_halo, image_halo = norm_back(halo_float, halo_inverse, grad_normed[1])
    gain_sum = gain_own + gain_halo
    small_own[...] = jnp.concatenate(
        [scale_sum, gain_sum[:, :OWN], gain_sum[:, OWN:], jnp.zeros((5, OWN), F32)], axis=0
    )
    remote(small_own, small_core, SMALL_CORE, sibling).start()

    start_plane(1)

    grad_send[...] = image_halo.astype(BF16)
    for place, step in reversed(tuple(zip(PLACES, OWNERS))):
        there = pl.ds(place[0], place[1])
        remote(grad_send.at[there], grad_back.at[there], BACK_SEM, neighbour(step)).start()

    start_line(0)

    wait_received(small_core, SMALL_CORE)
    chip_small = small_own[...] + small_core[...]
    small_plane[chip] = chip_small

    @pl.when(chip != 0)
    def _():
        remote(
            small_plane.at[chip], small_plane.at[chip], SMALL_PLANE, (z * 2, core)
        ).start()

    mixed = attended_t.T.astype(BF16)
    output_ref[...] = (own_float + dot(mixed, w_out_ref[...])).astype(BF16)

    start_line(1)

    @pl.when(chip == 0)
    def _():
        wait_received(small_plane.at[pl.ds(1, NP - 1)], SMALL_PLANE)
        plane = small_plane[0]
        for k in range(1, NP):
            plane = plane + small_plane[k]
        small_line[z] = plane

        slot = small_line.at[z]

        @pl.when(z >= OWNER_PLANES)
        def _():
            for k in range(OWNER_PLANES):
                remote(slot, slot, SMALL_LINE, z_id(k)).start()

        @pl.when(z < OWNER_PLANES)
        def _():
            remote(slot, slot, SMALL_LINE, z_id(1 - z)).start()

    wait_received(grad_back, BACK_SEM)
    grad_image = cot.astype(F32) + image_own
    grad_image = grad_image + dot(sel, grad_back[pl.ds(96, 128), :], ((0,), (0,)))
    top = grad_back[pl.ds(48, 48), :].astype(F32)
    bottom = grad_back[pl.ds(0, 48), :].astype(F32)
    grad_image = jnp.concatenate(
        [grad_image[:48] + top, grad_image[48:80], grad_image[80:] + bottom], axis=0
    )
    grad_image_ref[...] = grad_image.astype(BF16)

    start_gather()

    @pl.when(chip == 0)
    def _():
        @pl.when(z < OWNER_PLANES)
        def _():
            wait_received(small_line.at[pl.ds(0, NZ - 1)], SMALL_LINE)
            line = small_line[0]
            for k in range(1, NZ):
                line = line + small_line[k]
            small_total[...] = line * factor

        cast(small_total, SMALL_CAST, True)

        @pl.when(z >= OWNER_PLANES)
        def _():
            wait_received(small_total, SMALL_CAST)

        for other, device in peers:
            remote(small_total, small_total, SMALL_GATHER, device).start()

        cast(small_total, SMALL_CAST, False)

    cast(spot, CAST_SEM, False)

    wait_received(gathered.at[0, pl.ds(0, NP - 1)], GATHER_SEM)
    remote(own_half, own_half, BOTH_SEM, sibling).start()

    @pl.when(core == 0)
    def _():
        deliver_half(0)

    @pl.when(core == 1)
    def _():
        deliver_half(1)

    @pl.when(chip != 0)
    def _():
        wait_received(small_total, SMALL_GATHER)

    wait_received(gathered.at[1 - core], BOTH_SEM)

    @pl.when(core == 0)
    def _():
        deliver_half(1)

    @pl.when(core == 1)
    def _():
        deliver_half(0)

    wait_sent(halo, HALO_SEM)
    wait_sent(grad_send, BACK_SEM)
    wait_sent(small_own, SMALL_CORE)
    wait_sent(gathered.at[0, pl.ds(0, NP - 1)], GATHER_SEM)
    wait_sent(own_half, BOTH_SEM)
    for stage in range(2):
        wait_sent(core_send.at[stage], CORE_SEM + stage)
        wait_sent(plane_recv.at[stage], PLANE_SEM + stage)

    @pl.when(z >= OWNER_PLANES)
    def _():
        for stage in range(2):
            wait_sent(line_recv.at[stage, pl.ds(0, OWNER_PLANES)], LINE_SEM + stage)

    @pl.when(z < OWNER_PLANES)
    def _():
        for stage in range(2):
            wait_sent(line_send.at[stage], LINE_SEM + stage)

    for owner in range(OWNER_PLANES):

        @pl.when(z == owner)
        def _():
            wait_sent(gathered.at[0, pl.ds(0, len(CASTS[owner]))], CAST_SEM)

    @pl.when(chip != 0)
    def _():
        wait_sent(small_total, SMALL_PLANE)

    @pl.when(chip == 0)
    def _():
        wait_sent(small_plane.at[pl.ds(0, NP - 1)], SMALL_GATHER)

        @pl.when(z >= OWNER_PLANES)
        def _():
            wait_sent(small_line.at[pl.ds(0, OWNER_PLANES)], SMALL_LINE)

        @pl.when(z < OWNER_PLANES)
        def _():
            wait_sent(small_total, SMALL_LINE)

        for owner in range(OWNER_PLANES):

            @pl.when(z == owner)
            def _():
                wait_sent(small_line.at[pl.ds(0, len(CASTS[owner]))], SMALL_CAST)


def deliver(
    output,
    grad_image,
    grad_qkv,
    grad_out,
    small,
    output_out,
    grad_image_out,
    grad_qkv_out,
    grad_out_out,
    gain_out,
    scale_out,
    gain_ref,
    scale_ref,
    sems,
):
    steps = (
        (grad_qkv, grad_qkv_out),
        (grad_out, grad_out_out),
        (output, output_out),
        (grad_image, grad_image_out),
        (gain_ref, gain_out),
        (scale_ref, scale_out),
    )
    copies = [pltpu.make_async_copy(a, b, sems.at[i]) for i, (a, b) in enumerate(steps)]
    for copy in copies[:4]:
        copy.start()
    gain_ref[:, pl.ds(0, OWN)] = small[pl.ds(1, 1), :]
    gain_ref[:, pl.ds(OWN, OWN)] = small[pl.ds(2, 1), :]
    scale_ref[...] = small[pl.ds(0, 1), pl.ds(0, HEADS)]
    for copy in copies[4:]:
        copy.start()
    for copy in copies:
        copy.wait()


def on_device(image, w_qkv, w_out, norm_gain, head_scale, cotangent):
    rows = lax.axis_size("row")
    cols = lax.axis_size("col")
    vmem = pl.BlockSpec(memory_space=pltpu.VMEM)
    hbm = pl.BlockSpec(memory_space=pl.ANY)
    factor = 1.0 / math.sqrt(rows * TH * cols * TW)

    def kernel(*refs):
        block(rows, cols, factor, *refs)

    def pinned(array):
        return pltpu.with_memory_space_constraint(array, pltpu.HBM)

    parts = pl.pallas_call(
        kernel,
        out_shape=(
            pltpu.VMEM((OWN, C), BF16),
            pltpu.VMEM((OWN, C), BF16),
            pltpu.VMEM((C, 3 * C), F32),
            pltpu.VMEM((C, C), F32),
            pltpu.VMEM((8, OWN), F32),
        ),
        in_specs=[hbm] * 6,
        out_specs=(vmem,) * 5,
        scratch_shapes=[
            pltpu.VMEM((OWN, C), BF16),
            pltpu.VMEM((C, 3 * C), BF16),
            pltpu.VMEM((C, C), BF16),
            pltpu.VMEM((1, C), F32),
            pltpu.SMEM((1, HEADS), F32),
            pltpu.VMEM((OWN, C), BF16),
            pltpu.VMEM((HALO, C), BF16),
            pltpu.VMEM((OWN, C), BF16),
            pltpu.VMEM((HALO, C), BF16),
            pltpu.VMEM((HALO, C), BF16),
            pltpu.VMEM((C, LANES), BF16),
            pltpu.VMEM((C, LANES), BF16),
            pltpu.VMEM((4, C, C), F32),
            pltpu.VMEM((2, C, C), BF16),
            pltpu.VMEM((2, C, C), BF16),
            pltpu.VMEM((2, C, C), F32),
            pltpu.VMEM((2, C, C), BF16),
            pltpu.VMEM((2, NP - 1, 16, C), BF16),
            pltpu.VMEM((2, 16, C), BF16),
            pltpu.VMEM((2, NZ, 16, C), BF16),
            pltpu.VMEM((2, NP, 2, 16, C), BF16),
            pltpu.VMEM((8, OWN), F32),
            pltpu.VMEM((8, OWN), F32),
            pltpu.VMEM((NP, 8, OWN), F32),
            pltpu.VMEM((NZ, 8, OWN), F32),
            pltpu.SemaphoreType.DMA((32,)),
            pltpu.SemaphoreType.DMA((6,)),
        ],
        compiler_params=pltpu.CompilerParams(
            collective_id=0, has_side_effects=True, vmem_limit_bytes=VMEM_LIMIT
        ),
    )(
        *map(
            pinned,
            (
                image.reshape(OWN, C),
                w_qkv,
                w_out,
                norm_gain.reshape(1, C),
                head_scale.reshape(1, HEADS),
                cotangent.reshape(OWN, C),
            ),
        )
    )
    output, grad_image, grad_qkv, grad_out, grad_gain, grad_scale = pl.pallas_call(
        deliver,
        out_shape=(
            jax.ShapeDtypeStruct((OWN, C), BF16),
            jax.ShapeDtypeStruct((OWN, C), BF16),
            jax.ShapeDtypeStruct((C, 3 * C), F32),
            jax.ShapeDtypeStruct((C, C), F32),
            jax.ShapeDtypeStruct((1, C), F32),
            jax.ShapeDtypeStruct((1, HEADS), F32),
        ),
        in_specs=[vmem] * 5,
        out_specs=(hbm,) * 6,
        scratch_shapes=[
            pltpu.VMEM((1, C), F32),
            pltpu.VMEM((1, HEADS), F32),
            pltpu.SemaphoreType.DMA((6,)),
        ],
        compiler_params=pltpu.CompilerParams(vmem_limit_bytes=VMEM_LIMIT),
    )(*(pltpu.with_memory_space_constraint(part, pltpu.VMEM) for part in parts))
    return (
        output.reshape(TH, TW, C),
        grad_image.reshape(TH, TW, C),
        grad_qkv,
        grad_out,
        grad_gain.reshape(C),
        grad_scale.reshape(HEADS),
    )


def solution(mesh):
    placed = (P("row", "col", None), P(), P(), P(), P(), P("row", "col", None))
    return jax.shard_map(
        on_device,
        mesh=mesh,
        in_specs=placed,
        out_specs=(P("row", "col", None), P("row", "col", None), P(), P(), P(), P()),
        check_vma=False,
    )
```

```python
import math

import jax
import jax.numpy as jnp
from jax import lax
from jax.experimental import pallas as pl
from jax.experimental.pallas import tpu as pltpu
from jax.sharding import PartitionSpec as P

C = 256
HEADS = 4
HEAD_DIM = 64
RADIUS = 3
TH = 8
TW = 16
OWN = TH * TW
HALO = 224
KEYS = OWN + HALO
LANES = HEADS * OWN
EPS = 1e-06
NP = 16
VMEM_LIMIT = 40 * 1024 * 1024
NZ = 16
MESH = pl.DeviceIdType.MESH
F32 = jnp.float32
BF16 = jnp.bfloat16

PLACES = (
    (0, 48, -3, 0, 16),
    (48, 48, TH, 0, 16),
    (96, 32, 0, -3, 4),
    (128, 32, 0, TW, 4),
    (160, 16, -3, -3, 4),
    (176, 16, -3, TW, 4),
    (192, 16, TH, -3, 4),
    (208, 16, TH, TW, 4),
)
OWNERS = ((-1, 0), (1, 0), (0, -1), (0, 1), (-1, -1), (-1, 1), (1, -1), (1, 1))

STEPS = sorted(
    ((dx, dy) for dx in range(4) for dy in range(4) if dx or dy),
    key=lambda step: (-min(step[0], 4 - step[0]) - min(step[1], 4 - step[1]), step),
)
OWNER_PLANES = 2
CASTS = ((10, 11, 12, 13, 14, 15), (2, 3, 4, 5, 6, 7, 8, 9))
CASTS_FIRST = 4
HALO_SEM, BACK_SEM, SMALL_CORE, SMALL_PLANE, SMALL_LINE, SMALL_CAST, SMALL_GATHER = range(7)
CAST_SEM, GATHER_SEM, BOTH_SEM = range(7, 10)
CORE_SEM, PLANE_SEM, LINE_SEM = range(10, 16, 2)


def dot(a, b, contract=((1,), (0,))):
    return lax.dot_general(a, b, (contract, ((), ())), preferred_element_type=F32)


def key_mask(row, col, height, breadth):
    blocks = []
    for first, count, y0, x0, across in ((-1, OWN, 0, 0, TW),) + PLACES:
        place = lax.broadcasted_iota(jnp.int32, (count, OWN), 0)
        query = lax.broadcasted_iota(jnp.int32, (count, OWN), 1)
        y = place // across + y0
        x = place % across + x0
        ok = (jnp.abs(y - query // TW) <= RADIUS) & (jnp.abs(x - query % TW) <= RADIUS)
        gy = y + row * TH
        gx = x + col * TW
        ok = ok & (gy >= 0) & (gy < height) & (gx >= 0) & (gx < breadth)
        if across == 4:
            ok = ok & (place % 4 < RADIUS)
            if count == 16:
                ok = ok & (place // 4 < RADIUS)
        blocks.append(jnp.where(ok, 1.0, 0.0).astype(F32))
    return jnp.concatenate(blocks, axis=0)


def selection():
    blocks = []
    for first, count, y0, x0, across in PLACES[2:]:
        place = lax.broadcasted_iota(jnp.int32, (count, OWN), 0)
        pixel = lax.broadcasted_iota(jnp.int32, (count, OWN), 1)
        y = place // 4 + (y0 + TH) % TH
        x = place % 4 + (x0 + TW) % TW
        ok = (pixel == y * TW + x) & (place % 4 < RADIUS)
        if count == 16:
            ok = ok & (place // 4 < RADIUS)
        blocks.append(jnp.where(ok, 1.0, 0.0).astype(F32))
    return jnp.concatenate(blocks, axis=0).astype(BF16)


def block(rows, cols, factor, *refs):
    (
        image_hbm,
        w_qkv_hbm,
        w_out_hbm,
        gain_hbm,
        scale_hbm,
        cot_hbm,
        output_ref,
        grad_image_ref,
        grad_qkv_ref,
        grad_out_ref,
        small_total,
        image_ref,
        w_qkv_ref,
        w_out_ref,
        gain_ref,
        scale_ref,
        cot_ref,
        halo,
        side,
        grad_send,
        grad_back,
        q_block,
        g_block,
        total,
        core_send,
        core_recv,
        mine,
        plane_send,
        plane_recv,
        line_send,
        line_recv,
        gathered,
        small_own,
        small_core,
        small_plane,
        small_line,
        sems,
        local_sems,
    ) = refs
    row = lax.axis_index("row")
    col = lax.axis_index("col")
    z = row // 2
    core = col % 2
    x = (col // 8) * 2 + row % 2
    y = (col // 2) % 4
    chip = x * 4 + y
    sibling = (row, col + 1 - 2 * core)

    loads = []
    for i, (src, dst) in enumerate(
        (
            (image_hbm, image_ref),
            (w_qkv_hbm, w_qkv_ref),
            (cot_hbm, cot_ref),
            (w_out_hbm, w_out_ref),
            (gain_hbm, gain_ref),
            (scale_hbm, scale_ref),
        )
    ):
        load = pltpu.make_async_copy(src, dst, local_sems.at[i])
        load.start()
        loads.append(load)

    def chip_id(ox, oy):
        return (z * 2 + ox % 2, (ox // 2) * 8 + oy * 2 + core)

    def z_id(other):
        return (other * 2 + row % 2, col)

    def neighbour(step):
        return (lax.rem(row + step[0] + rows, rows), lax.rem(col + step[1] + cols, cols))

    peers = []
    for dx, dy in STEPS:
        ox, oy = lax.rem(x + dx, 4), lax.rem(y + dy, 4)
        peers.append((ox * 4 + oy, chip_id(ox, oy)))

    barrier = pltpu.get_barrier_semaphore()

    def greet(device):
        pl.semaphore_signal(barrier, inc=1, device_id=device, device_id_type=MESH)

    for step in OWNERS:
        greet(neighbour(step))
    for other, device in peers:
        greet(device)

    @pl.when(z < OWNER_PLANES)
    def _():
        for k in range(1, NZ):
            greet(z_id(lax.rem(z + k, NZ)))

    @pl.when(z >= OWNER_PLANES)
    def _():
        greet(z_id(jnp.where(z >= 10, 0, 1)))

    def remote(src, dst, sem, device):
        return pltpu.make_async_remote_copy(
            src_ref=src,
            dst_ref=dst,
            send_sem=sems.at[2 * sem],
            recv_sem=sems.at[2 * sem + 1],
            device_id=device,
            device_id_type=MESH,
        )

    def wait_sent(ref, sem):
        pltpu.make_async_copy(ref, ref, sems.at[2 * sem]).wait()

    def wait_received(ref, sem):
        pltpu.make_async_copy(ref, ref, sems.at[2 * sem + 1]).wait()

    sel = selection()
    loads[0].wait()
    side[...] = dot(sel, image_ref[...]).astype(BF16)

    @pl.when(z >= OWNER_PLANES)
    def _():
        pl.semaphore_wait(barrier, 8 + (NP - 1) + OWNER_PLANES)

    for owner in range(OWNER_PLANES):

        @pl.when(z == owner)
        def _():
            pl.semaphore_wait(barrier, 8 + (NP - 1) + 1 + len(CASTS[owner]))

    for place, step in reversed(tuple(zip(PLACES, OWNERS))):
        first, count = place[0], place[1]
        if first == 0:
            src = image_ref.at[pl.ds(OWN - 48, 48)]
        elif first == 48:
            src = image_ref.at[pl.ds(0, 48)]
        else:
            src = side.at[pl.ds(first - 96, count)]
        remote(
            src, halo.at[pl.ds(first, count)], HALO_SEM, neighbour((-step[0], -step[1]))
        ).start()

    for load in loads[1:]:
        load.wait()
    gain = gain_ref[...]
    w_q = w_qkv_ref[:, :C]
    w_kv = w_qkv_ref[:, C:]
    cot = cot_ref[...]
    mask = key_mask(row, col, rows * TH, cols * TW)

    def norm(values):
        inverse = lax.rsqrt(jnp.mean(values * values, axis=-1, keepdims=True) + EPS)
        return inverse, (values * inverse * gain).astype(BF16)

    own_float = image_ref[...].astype(F32)
    own_inverse, own_normed = norm(own_float)
    own_normed_t = own_normed.astype(F32).T.astype(BF16)
    query = dot(own_normed, w_q).astype(BF16)
    query_t = query.astype(F32).T
    q_block[...] = jnp.zeros_like(q_block)
    g_block[...] = jnp.zeros_like(g_block)
    grad_mixed_t = dot(w_out_ref[...], cot, ((1,), (1,)))
    q_inverse = []
    for h in range(HEADS):
        ch = slice(h * HEAD_DIM, (h + 1) * HEAD_DIM)
        ln = slice(h * OWN, (h + 1) * OWN)
        part = query_t[ch]
        q_block[ch, ln] = part.astype(BF16)
        g_block[ch, ln] = grad_mixed_t[ch].astype(BF16)
        q_inverse.append(lax.rsqrt(jnp.sum(part * part, axis=0, keepdims=True) + EPS))

    def segment(normed, mask_part):
        kv = dot(normed, w_kv).astype(BF16)
        keys = kv[:, :C]
        values = kv[:, C:]
        keys_float = keys.astype(F32)
        scores = dot(keys, q_block[...])
        weights = []
        logits = []
        inverses = []
        for h in range(HEADS):
            k_part = keys_float[:, h * HEAD_DIM : (h + 1) * HEAD_DIM]
            inverse = lax.rsqrt(jnp.sum(k_part * k_part, axis=1, keepdims=True) + EPS)
            logit = scores[:, h * OWN : (h + 1) * OWN] * inverse
            logit = logit * (q_inverse[h] * scale_ref[0, h])
            weights.append(jnp.exp(logit) * mask_part)
            logits.append(logit)
            inverses.append(inverse)
        keys_t = keys_float.T.astype(BF16)
        values_t = values.astype(F32).T.astype(BF16)
        grad_probs = dot(values, g_block[...])
        return keys_float, keys_t, values_t, weights, logits, inverses, grad_probs

    own_part = segment(own_normed, mask[:OWN])

    wait_received(halo, HALO_SEM)

    halo_float = halo[...].astype(F32)
    halo_inverse, halo_normed = norm(halo_float)
    halo_normed_t = halo_normed.astype(F32).T.astype(BF16)
    parts = (own_part, segment(halo_normed, mask[OWN:]))
    normed_t = (own_normed_t, halo_normed_t)
    probs = ([], [])
    probs_bf = ([], [])
    attended_t = []
    for h in range(HEADS):
        ch = slice(h * HEAD_DIM, (h + 1) * HEAD_DIM)
        weights = [part[3][h] for part in parts]
        weight_sum = sum(jnp.sum(weight, axis=0, keepdims=True) for weight in weights)
        inverse_sum = 1.0 / weight_sum
        mixed_head = 0.0
        for i in range(2):
            prob = weights[i] * inverse_sum
            probs[i].append(prob)
            probs_bf[i].append(prob.astype(BF16))
            mixed_head = mixed_head + dot(parts[i][2][ch], probs_bf[i][h])
        attended_t.append(mixed_head)
    attended_t = jnp.concatenate(attended_t, axis=0)
    grad_v = [
        dot(jnp.concatenate(probs_bf[i], axis=1), g_block[...], ((1,), (1,))).astype(BF16)
        for i in range(2)
    ]

    def start_core(stage):
        core_send[stage] = total[2 * stage + 1 - core].astype(BF16)
        remote(core_send.at[stage], core_recv.at[stage], CORE_SEM + stage, sibling).start()

    def start_plane(stage):
        wait_received(core_recv.at[stage], CORE_SEM + stage)
        summed = total[2 * stage + core] + core_recv[stage].astype(F32)
        mine[stage] = summed
        plane_send[stage] = summed.astype(BF16)
        for k, (other, device) in enumerate(peers):
            remote(
                plane_send.at[stage, pl.ds(pl.multiple_of(other * 16, 16), 16)],
                plane_recv.at[stage, k],
                PLANE_SEM + stage,
                device,
            ).start()

    def start_line(stage):
        fifteen = plane_recv.at[stage]
        wait_received(fifteen, PLANE_SEM + stage)
        summed = mine[stage, pl.ds(pl.multiple_of(chip * 16, 16), 16), :]
        for k in range(NP - 1):
            summed = summed + plane_recv[stage, k].astype(F32)

        summed = summed.astype(BF16)

        line_send[stage] = summed
        slot = line_recv.at[stage, z]

        @pl.when(z >= OWNER_PLANES)
        def _():
            for k in range(OWNER_PLANES):
                remote(line_send.at[stage], slot, LINE_SEM + stage, z_id(k)).start()

        @pl.when(z < OWNER_PLANES)
        def _():
            line_recv[stage, z] = summed
            remote(line_send.at[stage], slot, LINE_SEM + stage, z_id(1 - z)).start()

    def cast(ref, sem, first, last):
        for owner in range(OWNER_PLANES):

            @pl.when(z == owner)
            def _():
                for k in CASTS[owner][first:last]:
                    remote(ref, ref, sem, z_id(k)).start()

    spot = gathered.at[core, chip]
    own_half = gathered.at[core]

    def start_gather():
        @pl.when(z < OWNER_PLANES)
        def _():
            for stage in range(2):
                wait_received(line_recv.at[stage, pl.ds(0, NZ - 1)], LINE_SEM + stage)
                summed = line_recv[stage, 0].astype(F32)
                for k in range(1, NZ):
                    summed = summed + line_recv[stage, k].astype(F32)
                gathered[core, chip, stage] = (summed * factor).astype(BF16)

        @pl.when(z >= OWNER_PLANES)
        def _():
            wait_received(spot, CAST_SEM)

        for i, (other, device) in enumerate(peers):
            if i % 4 == 0:
                cast(spot, CAST_SEM, i // 4, i // 4 + 1)
            remote(spot, spot, GATHER_SEM, device).start()

    def deliver_half(side):
        values = [gathered[side, :, stage].reshape(C, C).astype(F32) for stage in range(2)]
        if side == 0:
            grad_qkv_ref[:, pl.ds(2 * C, C)] = values[0]
            grad_qkv_ref[:, pl.ds(0, C)] = values[1]
        else:
            grad_out_ref[...] = values[0]
            grad_qkv_ref[:, pl.ds(C, C)] = values[1]

    mixed_t = attended_t.astype(BF16)
    total[0] = dot(normed_t[0], grad_v[0]) + dot(normed_t[1], grad_v[1])
    total[1] = dot(mixed_t, cot)
    start_core(0)

    grad_logits = ([], [])
    k_along = ([], [])
    grad_q_t = []
    scale_sum = jnp.zeros((1, OWN), F32)
    lane = lax.broadcasted_iota(jnp.int32, (1, OWN), 1)
    for h in range(HEADS):
        ch = slice(h * HEAD_DIM, (h + 1) * HEAD_DIM)
        ln = slice(h * OWN, (h + 1) * OWN)
        scale = scale_ref[0, h]
        grad_probs = [part[6][:, ln] for part in parts]
        row_dot = sum(
            jnp.sum(probs[i][h] * grad_probs[i], axis=0, keepdims=True) for i in range(2)
        )
        along_q = 0.0
        unit_grad = 0.0
        for i in range(2):
            grad_logit = probs[i][h] * (grad_probs[i] - row_dot)
            product = grad_logit * parts[i][4][h]
            along_q = along_q + jnp.sum(product, axis=0, keepdims=True)
            k_along[i].append(jnp.sum(product, axis=1, keepdims=True))
            grad_logits[i].append((grad_logit * (q_inverse[h] * scale)).astype(BF16))
            unit_grad = unit_grad + dot(
                parts[i][1][ch], (grad_logit * (parts[i][5][h] * scale)).astype(BF16)
            )
        scale_sum = scale_sum + jnp.where(
            lane == h, jnp.sum(along_q, axis=1, keepdims=True) / scale, 0.0
        )
        grad_q_t.append(
            q_inverse[h] * (unit_grad - query_t[ch] * (q_inverse[h] * along_q))
        )

    start_plane(0)
    grad_q = jnp.concatenate(grad_q_t, axis=0).T.astype(BF16)
    low = lax.broadcasted_iota(jnp.int32, (1, OWN), 1) < HEAD_DIM
    grad_k = []
    for i in range(2):
        unit_grad = dot(jnp.concatenate(grad_logits[i], axis=1), q_block[...], ((1,), (1,)))
        keys_float, inverses = parts[i][0], parts[i][5]
        pieces = []
        for t in range(2):
            ln = slice(t * OWN, (t + 1) * OWN)
            inv = jnp.where(low, inverses[2 * t], inverses[2 * t + 1])
            along = jnp.where(low, k_along[i][2 * t], k_along[i][2 * t + 1])
            pieces.append(inv * (unit_grad[:, ln] - keys_float[:, ln] * (inv * along)))
        grad_k.append(jnp.concatenate(pieces, axis=1).astype(BF16))

    total[2] = dot(own_normed_t, grad_q)
    total[3] = dot(normed_t[0], grad_k[0]) + dot(normed_t[1], grad_k[1])
    start_core(1)

    grad_normed = [
        dot(jnp.concatenate([grad_k[i], grad_v[i]], axis=1), w_kv, ((1,), (1,)))
        for i in range(2)
    ]
    grad_normed[0] = grad_normed[0] + dot(grad_q, w_q, ((1,), (1,)))

    def norm_back(values, inverse, grad):
        scaled = values * inverse
        gain_term = jnp.sum(grad * scaled, axis=0, keepdims=True)
        grad = grad * gain
        along = jnp.mean(grad * scaled, axis=-1, keepdims=True)
        return gain_term, inverse * (grad - scaled * along)

    gain_own, image_own = norm_back(own_float, own_inverse, grad_normed[0])
    gain_halo, image_halo = norm_back(halo_float, halo_inverse, grad_normed[1])
    gain_sum = gain_own + gain_halo
    small_own[...] = jnp.concatenate(
        [scale_sum, gain_sum[:, :OWN], gain_sum[:, OWN:], jnp.zeros((5, OWN), F32)], axis=0
    )
    remote(small_own, small_core, SMALL_CORE, sibling).start()

    start_plane(1)

    grad_send[...] = image_halo.astype(BF16)
    for place, step in reversed(tuple(zip(PLACES, OWNERS))):
        there = pl.ds(place[0], place[1])
        remote(grad_send.at[there], grad_back.at[there], BACK_SEM, neighbour(step)).start()

    start_line(0)

    wait_received(small_core, SMALL_CORE)
    chip_small = small_own[...] + small_core[...]
    small_plane[chip] = chip_small

    @pl.when(chip != 0)
    def _():
        remote(
            small_plane.at[chip], small_plane.at[chip], SMALL_PLANE, (z * 2, core)
        ).start()

    mixed = attended_t.T.astype(BF16)
    output_ref[...] = (own_float + dot(mixed, w_out_ref[...])).astype(BF16)

    start_line(1)

    @pl.when(chip == 0)
    def _():
        wait_received(small_plane.at[pl.ds(1, NP - 1)], SMALL_PLANE)
        plane = small_plane[0]
        for k in range(1, NP):
            plane = plane + small_plane[k]
        small_line[z] = plane

        slot = small_line.at[z]

        @pl.when(z >= OWNER_PLANES)
        def _():
            for k in range(OWNER_PLANES):
                remote(slot, slot, SMALL_LINE, z_id(k)).start()

        @pl.when(z < OWNER_PLANES)
        def _():
            remote(slot, slot, SMALL_LINE, z_id(1 - z)).start()

    wait_received(grad_back, BACK_SEM)
    grad_image = cot.astype(F32) + image_own
    grad_image = grad_image + dot(sel, grad_back[pl.ds(96, 128), :], ((0,), (0,)))
    top = grad_back[pl.ds(48, 48), :].astype(F32)
    bottom = grad_back[pl.ds(0, 48), :].astype(F32)
    grad_image = jnp.concatenate(
        [grad_image[:48] + top, grad_image[48:80], grad_image[80:] + bottom], axis=0
    )
    grad_image_ref[...] = grad_image.astype(BF16)

    start_gather()
    cast(spot, CAST_SEM, CASTS_FIRST, NZ)

    @pl.when(chip == 0)
    def _():
        @pl.when(z < OWNER_PLANES)
        def _():
            wait_received(small_line.at[pl.ds(0, NZ - 1)], SMALL_LINE)
            line = small_line[0]
            for k in range(1, NZ):
                line = line + small_line[k]
            small_total[...] = line * factor

        cast(small_total, SMALL_CAST, 0, CASTS_FIRST)

        @pl.when(z >= OWNER_PLANES)
        def _():
            wait_received(small_total, SMALL_CAST)

        for other, device in peers:
            remote(small_total, small_total, SMALL_GATHER, device).start()

        cast(small_total, SMALL_CAST, CASTS_FIRST, NZ)

    wait_received(gathered.at[0, pl.ds(0, NP - 1)], GATHER_SEM)
    remote(own_half, own_half, BOTH_SEM, sibling).start()

    @pl.when(core == 0)
    def _():
        deliver_half(0)

    @pl.when(core == 1)
    def _():
        deliver_half(1)

    @pl.when(chip != 0)
    def _():
        wait_received(small_total, SMALL_GATHER)

    wait_received(gathered.at[1 - core], BOTH_SEM)

    @pl.when(core == 0)
    def _():
        deliver_half(1)

    @pl.when(core == 1)
    def _():
        deliver_half(0)

    wait_sent(halo, HALO_SEM)
    wait_sent(grad_send, BACK_SEM)
    wait_sent(small_own, SMALL_CORE)
    wait_sent(gathered.at[0, pl.ds(0, NP - 1)], GATHER_SEM)
    wait_sent(own_half, BOTH_SEM)
    for stage in range(2):
        wait_sent(core_send.at[stage], CORE_SEM + stage)
        wait_sent(plane_recv.at[stage], PLANE_SEM + stage)

    @pl.when(z >= OWNER_PLANES)
    def _():
        for stage in range(2):
            wait_sent(line_recv.at[stage, pl.ds(0, OWNER_PLANES)], LINE_SEM + stage)

    @pl.when(z < OWNER_PLANES)
    def _():
        for stage in range(2):
            wait_sent(line_send.at[stage], LINE_SEM + stage)

    for owner in range(OWNER_PLANES):

        @pl.when(z == owner)
        def _():
            wait_sent(gathered.at[0, pl.ds(0, len(CASTS[owner]))], CAST_SEM)

    @pl.when(chip != 0)
    def _():
        wait_sent(small_total, SMALL_PLANE)

    @pl.when(chip == 0)
    def _():
        wait_sent(small_plane.at[pl.ds(0, NP - 1)], SMALL_GATHER)

        @pl.when(z >= OWNER_PLANES)
        def _():
            wait_sent(small_line.at[pl.ds(0, OWNER_PLANES)], SMALL_LINE)

        @pl.when(z < OWNER_PLANES)
        def _():
            wait_sent(small_total, SMALL_LINE)

        for owner in range(OWNER_PLANES):

            @pl.when(z == owner)
            def _():
                wait_sent(small_line.at[pl.ds(0, len(CASTS[owner]))], SMALL_CAST)


def deliver(
    output,
    grad_image,
    grad_qkv,
    grad_out,
    small,
    output_out,
    grad_image_out,
    grad_qkv_out,
    grad_out_out,
    gain_out,
    scale_out,
    gain_ref,
    scale_ref,
    sems,
):
    steps = (
        (grad_qkv, grad_qkv_out),
        (grad_out, grad_out_out),
        (output, output_out),
        (grad_image, grad_image_out),
        (gain_ref, gain_out),
        (scale_ref, scale_out),
    )
    copies = [pltpu.make_async_copy(a, b, sems.at[i]) for i, (a, b) in enumerate(steps)]
    for copy in copies[:4]:
        copy.start()
    gain_ref[:, pl.ds(0, OWN)] = small[pl.ds(1, 1), :]
    gain_ref[:, pl.ds(OWN, OWN)] = small[pl.ds(2, 1), :]
    scale_ref[...] = small[pl.ds(0, 1), pl.ds(0, HEADS)]
    for copy in copies[4:]:
        copy.start()
    for copy in copies:
        copy.wait()


def on_device(image, w_qkv, w_out, norm_gain, head_scale, cotangent):
    rows = lax.axis_size("row")
    cols = lax.axis_size("col")
    vmem = pl.BlockSpec(memory_space=pltpu.VMEM)
    hbm = pl.BlockSpec(memory_space=pl.ANY)
    factor = 1.0 / math.sqrt(rows * TH * cols * TW)

    def kernel(*refs):
        block(rows, cols, factor, *refs)

    def pinned(array):
        return pltpu.with_memory_space_constraint(array, pltpu.HBM)

    parts = pl.pallas_call(
        kernel,
        out_shape=(
            pltpu.VMEM((OWN, C), BF16),
            pltpu.VMEM((OWN, C), BF16),
            pltpu.VMEM((C, 3 * C), F32),
            pltpu.VMEM((C, C), F32),
            pltpu.VMEM((8, OWN), F32),
        ),
        in_specs=[hbm] * 6,
        out_specs=(vmem,) * 5,
        scratch_shapes=[
            pltpu.VMEM((OWN, C), BF16),
            pltpu.VMEM((C, 3 * C), BF16),
            pltpu.VMEM((C, C), BF16),
            pltpu.VMEM((1, C), F32),
            pltpu.SMEM((1, HEADS), F32),
            pltpu.VMEM((OWN, C), BF16),
            pltpu.VMEM((HALO, C), BF16),
            pltpu.VMEM((OWN, C), BF16),
            pltpu.VMEM((HALO, C), BF16),
            pltpu.VMEM((HALO, C), BF16),
            pltpu.VMEM((C, LANES), BF16),
            pltpu.VMEM((C, LANES), BF16),
            pltpu.VMEM((4, C, C), F32),
            pltpu.VMEM((2, C, C), BF16),
            pltpu.VMEM((2, C, C), BF16),
            pltpu.VMEM((2, C, C), F32),
            pltpu.VMEM((2, C, C), BF16),
            pltpu.VMEM((2, NP - 1, 16, C), BF16),
            pltpu.VMEM((2, 16, C), BF16),
            pltpu.VMEM((2, NZ, 16, C), BF16),
            pltpu.VMEM((2, NP, 2, 16, C), BF16),
            pltpu.VMEM((8, OWN), F32),
            pltpu.VMEM((8, OWN), F32),
            pltpu.VMEM((NP, 8, OWN), F32),
            pltpu.VMEM((NZ, 8, OWN), F32),
            pltpu.SemaphoreType.DMA((32,)),
            pltpu.SemaphoreType.DMA((6,)),
        ],
        compiler_params=pltpu.CompilerParams(
            collective_id=0, has_side_effects=True, vmem_limit_bytes=VMEM_LIMIT
        ),
    )(
        *map(
            pinned,
            (
                image.reshape(OWN, C),
                w_qkv,
                w_out,
                norm_gain.reshape(1, C),
                head_scale.reshape(1, HEADS),
                cotangent.reshape(OWN, C),
            ),
        )
    )
    output, grad_image, grad_qkv, grad_out, grad_gain, grad_scale = pl.pallas_call(
        deliver,
        out_shape=(
            jax.ShapeDtypeStruct((OWN, C), BF16),
            jax.ShapeDtypeStruct((OWN, C), BF16),
            jax.ShapeDtypeStruct((C, 3 * C), F32),
            jax.ShapeDtypeStruct((C, C), F32),
            jax.ShapeDtypeStruct((1, C), F32),
            jax.ShapeDtypeStruct((1, HEADS), F32),
        ),
        in_specs=[vmem] * 5,
        out_specs=(hbm,) * 6,
        scratch_shapes=[
            pltpu.VMEM((1, C), F32),
            pltpu.VMEM((1, HEADS), F32),
            pltpu.SemaphoreType.DMA((6,)),
        ],
        compiler_params=pltpu.CompilerParams(vmem_limit_bytes=VMEM_LIMIT),
    )(*(pltpu.with_memory_space_constraint(part, pltpu.VMEM) for part in parts))
    return (
        output.reshape(TH, TW, C),
        grad_image.reshape(TH, TW, C),
        grad_qkv,
        grad_out,
        grad_gain.reshape(C),
        grad_scale.reshape(HEADS),
    )


def solution(mesh):
    placed = (P("row", "col", None), P(), P(), P(), P(), P("row", "col", None))
    return jax.shard_map(
        on_device,
        mesh=mesh,
        in_specs=placed,
        out_specs=(P("row", "col", None), P("row", "col", None), P(), P(), P(), P()),
        check_vma=False,
    )
```

```python
import math

import jax
import jax.numpy as jnp
from jax import lax
from jax.experimental import pallas as pl
from jax.experimental.pallas import tpu as pltpu
from jax.sharding import PartitionSpec as P

C = 256
HEADS = 4
HEAD_DIM = 64
RADIUS = 3
TH = 8
TW = 16
OWN = TH * TW
HALO = 224
KEYS = OWN + HALO
LANES = HEADS * OWN
EPS = 1e-06
NP = 16
VMEM_LIMIT = 40 * 1024 * 1024
NZ = 16
MESH = pl.DeviceIdType.MESH
F32 = jnp.float32
BF16 = jnp.bfloat16

PLACES = (
    (0, 48, -3, 0, 16),
    (48, 48, TH, 0, 16),
    (96, 32, 0, -3, 4),
    (128, 32, 0, TW, 4),
    (160, 16, -3, -3, 4),
    (176, 16, -3, TW, 4),
    (192, 16, TH, -3, 4),
    (208, 16, TH, TW, 4),
)
OWNERS = ((-1, 0), (1, 0), (0, -1), (0, 1), (-1, -1), (-1, 1), (1, -1), (1, 1))

STEPS = sorted(
    ((dx, dy) for dx in range(4) for dy in range(4) if dx or dy),
    key=lambda step: (-min(step[0], 4 - step[0]) - min(step[1], 4 - step[1]), step),
)
OWNER_PLANES = 2
CASTS = ((10, 11, 12, 13, 14, 15), (2, 3, 4, 5, 6, 7, 8, 9))
CASTS_FIRST = 4
HALO_SEM, BACK_SEM, SMALL_CORE, SMALL_PLANE, SMALL_LINE, SMALL_CAST, SMALL_GATHER = range(7)
CAST_SEM, GATHER_SEM, BOTH_SEM = range(7, 10)
CORE_SEM, PLANE_SEM, LINE_SEM = range(10, 16, 2)


def dot(a, b, contract=((1,), (0,))):
    return lax.dot_general(a, b, (contract, ((), ())), preferred_element_type=F32)


def key_mask(row, col, height, breadth):
    blocks = []
    for first, count, y0, x0, across in ((-1, OWN, 0, 0, TW),) + PLACES:
        place = lax.broadcasted_iota(jnp.int32, (count, OWN), 0)
        query = lax.broadcasted_iota(jnp.int32, (count, OWN), 1)
        y = place // across + y0
        x = place % across + x0
        ok = (jnp.abs(y - query // TW) <= RADIUS) & (jnp.abs(x - query % TW) <= RADIUS)
        gy = y + row * TH
        gx = x + col * TW
        ok = ok & (gy >= 0) & (gy < height) & (gx >= 0) & (gx < breadth)
        if across == 4:
            ok = ok & (place % 4 < RADIUS)
            if count == 16:
                ok = ok & (place // 4 < RADIUS)
        blocks.append(jnp.where(ok, 1.0, 0.0).astype(F32))
    return jnp.concatenate(blocks, axis=0)


def selection():
    blocks = []
    for first, count, y0, x0, across in PLACES[2:]:
        place = lax.broadcasted_iota(jnp.int32, (count, OWN), 0)
        pixel = lax.broadcasted_iota(jnp.int32, (count, OWN), 1)
        y = place // 4 + (y0 + TH) % TH
        x = place % 4 + (x0 + TW) % TW
        ok = (pixel == y * TW + x) & (place % 4 < RADIUS)
        if count == 16:
            ok = ok & (place // 4 < RADIUS)
        blocks.append(jnp.where(ok, 1.0, 0.0).astype(F32))
    return jnp.concatenate(blocks, axis=0).astype(BF16)


def block(rows, cols, factor, *refs):
    (
        image_hbm,
        w_qkv_hbm,
        w_out_hbm,
        gain_hbm,
        scale_hbm,
        cot_hbm,
        output_ref,
        grad_image_ref,
        grad_qkv_ref,
        grad_out_ref,
        small_total,
        image_ref,
        w_qkv_ref,
        w_out_ref,
        gain_ref,
        scale_ref,
        cot_ref,
        halo,
        side,
        grad_send,
        grad_back,
        q_block,
        g_block,
        total,
        core_send,
        core_recv,
        mine,
        plane_send,
        plane_recv,
        line_send,
        line_recv,
        gathered,
        small_own,
        small_core,
        small_plane,
        small_line,
        sems,
        local_sems,
    ) = refs
    row = lax.axis_index("row")
    col = lax.axis_index("col")
    z = row // 2
    core = col % 2
    x = (col // 8) * 2 + row % 2
    y = (col // 2) % 4
    chip = x * 4 + y
    sibling = (row, col + 1 - 2 * core)

    loads = []
    for i, (src, dst) in enumerate(
        (
            (image_hbm, image_ref),
            (w_qkv_hbm, w_qkv_ref),
            (cot_hbm, cot_ref),
            (w_out_hbm, w_out_ref),
            (gain_hbm, gain_ref),
            (scale_hbm, scale_ref),
        )
    ):
        load = pltpu.make_async_copy(src, dst, local_sems.at[i])
        load.start()
        loads.append(load)

    def chip_id(ox, oy):
        return (z * 2 + ox % 2, (ox // 2) * 8 + oy * 2 + core)

    def z_id(other):
        return (other * 2 + row % 2, col)

    def neighbour(step):
        return (lax.rem(row + step[0] + rows, rows), lax.rem(col + step[1] + cols, cols))

    peers = []
    for dx, dy in STEPS:
        ox, oy = lax.rem(x + dx, 4), lax.rem(y + dy, 4)
        peers.append((ox * 4 + oy, chip_id(ox, oy)))

    barrier = pltpu.get_barrier_semaphore()

    def greet(device):
        pl.semaphore_signal(barrier, inc=1, device_id=device, device_id_type=MESH)

    for step in OWNERS:
        greet(neighbour(step))
    for other, device in peers:
        greet(device)

    @pl.when(z < OWNER_PLANES)
    def _():
        for k in range(1, NZ):
            greet(z_id(lax.rem(z + k, NZ)))

    def remote(src, dst, sem, device):
        return pltpu.make_async_remote_copy(
            src_ref=src,
            dst_ref=dst,
            send_sem=sems.at[2 * sem],
            recv_sem=sems.at[2 * sem + 1],
            device_id=device,
            device_id_type=MESH,
        )

    def wait_sent(ref, sem):
        pltpu.make_async_copy(ref, ref, sems.at[2 * sem]).wait()

    def wait_received(ref, sem):
        pltpu.make_async_copy(ref, ref, sems.at[2 * sem + 1]).wait()

    sel = selection()
    loads[0].wait()
    side[...] = dot(sel, image_ref[...]).astype(BF16)

    owners = OWNER_PLANES - jnp.where(z < OWNER_PLANES, 1, 0)
    pl.semaphore_wait(barrier, 8 + (NP - 1) + owners)

    for place, step in reversed(tuple(zip(PLACES, OWNERS))):
        first, count = place[0], place[1]
        if first == 0:
            src = image_ref.at[pl.ds(OWN - 48, 48)]
        elif first == 48:
            src = image_ref.at[pl.ds(0, 48)]
        else:
            src = side.at[pl.ds(first - 96, count)]
        remote(
            src, halo.at[pl.ds(first, count)], HALO_SEM, neighbour((-step[0], -step[1]))
        ).start()

    for load in loads[1:]:
        load.wait()
    gain = gain_ref[...]
    w_q = w_qkv_ref[:, :C]
    w_kv = w_qkv_ref[:, C:]
    cot = cot_ref[...]
    mask = key_mask(row, col, rows * TH, cols * TW)

    def norm(values):
        inverse = lax.rsqrt(jnp.mean(values * values, axis=-1, keepdims=True) + EPS)
        return inverse, (values * inverse * gain).astype(BF16)

    own_float = image_ref[...].astype(F32)
    own_inverse, own_normed = norm(own_float)
    own_normed_t = own_normed.astype(F32).T.astype(BF16)
    query = dot(own_normed, w_q).astype(BF16)
    query_t = query.astype(F32).T
    q_block[...] = jnp.zeros_like(q_block)
    g_block[...] = jnp.zeros_like(g_block)
    grad_mixed_t = dot(w_out_ref[...], cot, ((1,), (1,)))
    q_inverse = []
    for h in range(HEADS):
        ch = slice(h * HEAD_DIM, (h + 1) * HEAD_DIM)
        ln = slice(h * OWN, (h + 1) * OWN)
        part = query_t[ch]
        q_block[ch, ln] = part.astype(BF16)
        g_block[ch, ln] = grad_mixed_t[ch].astype(BF16)
        q_inverse.append(lax.rsqrt(jnp.sum(part * part, axis=0, keepdims=True) + EPS))

    def segment(normed, mask_part):
        kv = dot(normed, w_kv).astype(BF16)
        keys = kv[:, :C]
        values = kv[:, C:]
        keys_float = keys.astype(F32)
        scores = dot(keys, q_block[...])
        weights = []
        logits = []
        inverses = []
        for h in range(HEADS):
            k_part = keys_float[:, h * HEAD_DIM : (h + 1) * HEAD_DIM]
            inverse = lax.rsqrt(jnp.sum(k_part * k_part, axis=1, keepdims=True) + EPS)
            logit = scores[:, h * OWN : (h + 1) * OWN] * inverse
            logit = logit * (q_inverse[h] * scale_ref[0, h])
            weights.append(jnp.exp(logit) * mask_part)
            logits.append(logit)
            inverses.append(inverse)
        keys_t = keys_float.T.astype(BF16)
        values_t = values.astype(F32).T.astype(BF16)
        grad_probs = dot(values, g_block[...])
        return keys_float, keys_t, values_t, weights, logits, inverses, grad_probs

    own_part = segment(own_normed, mask[:OWN])

    wait_received(halo, HALO_SEM)

    halo_float = halo[...].astype(F32)
    halo_inverse, halo_normed = norm(halo_float)
    halo_normed_t = halo_normed.astype(F32).T.astype(BF16)
    parts = (own_part, segment(halo_normed, mask[OWN:]))
    normed_t = (own_normed_t, halo_normed_t)
    probs = ([], [])
    probs_bf = ([], [])
    attended_t = []
    for h in range(HEADS):
        ch = slice(h * HEAD_DIM, (h + 1) * HEAD_DIM)
        weights = [part[3][h] for part in parts]
        weight_sum = sum(jnp.sum(weight, axis=0, keepdims=True) for weight in weights)
        inverse_sum = 1.0 / weight_sum
        mixed_head = 0.0
        for i in range(2):
            prob = weights[i] * inverse_sum
            probs[i].append(prob)
            probs_bf[i].append(prob.astype(BF16))
            mixed_head = mixed_head + dot(parts[i][2][ch], probs_bf[i][h])
        attended_t.append(mixed_head)
    attended_t = jnp.concatenate(attended_t, axis=0)
    grad_v = [
        dot(jnp.concatenate(probs_bf[i], axis=1), g_block[...], ((1,), (1,))).astype(BF16)
        for i in range(2)
    ]

    def start_core(stage):
        core_send[stage] = total[2 * stage + 1 - core].astype(BF16)
        remote(core_send.at[stage], core_recv.at[stage], CORE_SEM + stage, sibling).start()

    def start_plane(stage):
        wait_received(core_recv.at[stage], CORE_SEM + stage)
        summed = total[2 * stage + core] + core_recv[stage].astype(F32)
        mine[stage] = summed
        plane_send[stage] = summed.astype(BF16)
        for k, (other, device) in enumerate(peers):
            remote(
                plane_send.at[stage, pl.ds(pl.multiple_of(other * 16, 16), 16)],
                plane_recv.at[stage, k],
                PLANE_SEM + stage,
                device,
            ).start()

    def start_line(stage):
        fifteen = plane_recv.at[stage]
        wait_received(fifteen, PLANE_SEM + stage)
        summed = mine[stage, pl.ds(pl.multiple_of(chip * 16, 16), 16), :]
        for k in range(NP - 1):
            summed = summed + plane_recv[stage, k].astype(F32)

        summed = summed.astype(BF16)

        line_send[stage] = summed
        slot = line_recv.at[stage, z]

        @pl.when(z >= OWNER_PLANES)
        def _():
            for k in range(OWNER_PLANES):
                remote(line_send.at[stage], slot, LINE_SEM + stage, z_id(k)).start()

        @pl.when(z < OWNER_PLANES)
        def _():
            line_recv[stage, z] = summed
            remote(line_send.at[stage], slot, LINE_SEM + stage, z_id(1 - z)).start()

    def cast(ref, sem, first, last):
        for owner in range(OWNER_PLANES):

            @pl.when(z == owner)
            def _():
                for k in CASTS[owner][first:last]:
                    remote(ref, ref, sem, z_id(k)).start()

    spot = gathered.at[core, chip]
    own_half = gathered.at[core]

    def start_gather():
        @pl.when(z < OWNER_PLANES)
        def _():
            for stage in range(2):
                wait_received(line_recv.at[stage, pl.ds(0, NZ - 1)], LINE_SEM + stage)
                summed = line_recv[stage, 0].astype(F32)
                for k in range(1, NZ):
                    summed = summed + line_recv[stage, k].astype(F32)
                gathered[core, chip, stage] = (summed * factor).astype(BF16)

        @pl.when(z >= OWNER_PLANES)
        def _():
            wait_received(spot, CAST_SEM)

        for i, (other, device) in enumerate(peers):
            if i % 4 == 0:
                cast(spot, CAST_SEM, i // 4, i // 4 + 1)
            remote(spot, spot, GATHER_SEM, device).start()

    def deliver_half(side):
        values = [gathered[side, :, stage].reshape(C, C).astype(F32) for stage in range(2)]
        if side == 0:
            grad_qkv_ref[:, pl.ds(2 * C, C)] = values[0]
            grad_qkv_ref[:, pl.ds(0, C)] = values[1]
        else:
            grad_out_ref[...] = values[0]
            grad_qkv_ref[:, pl.ds(C, C)] = values[1]

    mixed_t = attended_t.astype(BF16)
    total[0] = dot(normed_t[0], grad_v[0]) + dot(normed_t[1], grad_v[1])
    total[1] = dot(mixed_t, cot)
    start_core(0)

    grad_logits = ([], [])
    k_along = ([], [])
    grad_q_t = []
    scale_sum = jnp.zeros((1, OWN), F32)
    lane = lax.broadcasted_iota(jnp.int32, (1, OWN), 1)
    for h in range(HEADS):
        ch = slice(h * HEAD_DIM, (h + 1) * HEAD_DIM)
        ln = slice(h * OWN, (h + 1) * OWN)
        scale = scale_ref[0, h]
        grad_probs = [part[6][:, ln] for part in parts]
        row_dot = sum(
            jnp.sum(probs[i][h] * grad_probs[i], axis=0, keepdims=True) for i in range(2)
        )
        along_q = 0.0
        unit_grad = 0.0
        for i in range(2):
            grad_logit = probs[i][h] * (grad_probs[i] - row_dot)
            product = grad_logit * parts[i][4][h]
            along_q = along_q + jnp.sum(product, axis=0, keepdims=True)
            k_along[i].append(jnp.sum(product, axis=1, keepdims=True))
            grad_logits[i].append((grad_logit * (q_inverse[h] * scale)).astype(BF16))
            unit_grad = unit_grad + dot(
                parts[i][1][ch], (grad_logit * (parts[i][5][h] * scale)).astype(BF16)
            )
        scale_sum = scale_sum + jnp.where(
            lane == h, jnp.sum(along_q, axis=1, keepdims=True) / scale, 0.0
        )
        grad_q_t.append(
            q_inverse[h] * (unit_grad - query_t[ch] * (q_inverse[h] * along_q))
        )

    start_plane(0)
    grad_q = jnp.concatenate(grad_q_t, axis=0).T.astype(BF16)
    low = lax.broadcasted_iota(jnp.int32, (1, OWN), 1) < HEAD_DIM
    grad_k = []
    for i in range(2):
        unit_grad = dot(jnp.concatenate(grad_logits[i], axis=1), q_block[...], ((1,), (1,)))
        keys_float, inverses = parts[i][0], parts[i][5]
        pieces = []
        for t in range(2):
            ln = slice(t * OWN, (t + 1) * OWN)
            inv = jnp.where(low, inverses[2 * t], inverses[2 * t + 1])
            along = jnp.where(low, k_along[i][2 * t], k_along[i][2 * t + 1])
            pieces.append(inv * (unit_grad[:, ln] - keys_float[:, ln] * (inv * along)))
        grad_k.append(jnp.concatenate(pieces, axis=1).astype(BF16))

    total[2] = dot(own_normed_t, grad_q)
    total[3] = dot(normed_t[0], grad_k[0]) + dot(normed_t[1], grad_k[1])
    start_core(1)

    grad_normed = [
        dot(jnp.concatenate([grad_k[i], grad_v[i]], axis=1), w_kv, ((1,), (1,)))
        for i in range(2)
    ]
    grad_normed[0] = grad_normed[0] + dot(grad_q, w_q, ((1,), (1,)))

    def norm_back(values, inverse, grad):
        scaled = values * inverse
        gain_term = jnp.sum(grad * scaled, axis=0, keepdims=True)
        grad = grad * gain
        along = jnp.mean(grad * scaled, axis=-1, keepdims=True)
        return gain_term, inverse * (grad - scaled * along)

    gain_own, image_own = norm_back(own_float, own_inverse, grad_normed[0])
    gain_halo, image_halo = norm_back(halo_float, halo_inverse, grad_normed[1])
    gain_sum = gain_own + gain_halo
    small_own[...] = jnp.concatenate(
        [scale_sum, gain_sum[:, :OWN], gain_sum[:, OWN:], jnp.zeros((5, OWN), F32)], axis=0
    )
    remote(small_own, small_core, SMALL_CORE, sibling).start()

    start_plane(1)

    grad_send[...] = image_halo.astype(BF16)
    for place, step in reversed(tuple(zip(PLACES, OWNERS))):
        there = pl.ds(place[0], place[1])
        remote(grad_send.at[there], grad_back.at[there], BACK_SEM, neighbour(step)).start()

    start_line(0)

    wait_received(small_core, SMALL_CORE)
    chip_small = small_own[...] + small_core[...]
    small_plane[chip] = chip_small

    @pl.when(chip != 0)
    def _():
        remote(
            small_plane.at[chip], small_plane.at[chip], SMALL_PLANE, (z * 2, core)
        ).start()

    mixed = attended_t.T.astype(BF16)
    output_ref[...] = (own_float + dot(mixed, w_out_ref[...])).astype(BF16)

    start_line(1)

    @pl.when(chip == 0)
    def _():
        wait_received(small_plane.at[pl.ds(1, NP - 1)], SMALL_PLANE)
        plane = small_plane[0]
        for k in range(1, NP):
            plane = plane + small_plane[k]
        small_line[z] = plane

        slot = small_line.at[z]

        @pl.when(z >= OWNER_PLANES)
        def _():
            for k in range(OWNER_PLANES):
                remote(slot, slot, SMALL_LINE, z_id(k)).start()

        @pl.when(z < OWNER_PLANES)
        def _():
            remote(slot, slot, SMALL_LINE, z_id(1 - z)).start()

    wait_received(grad_back, BACK_SEM)
    grad_image = cot.astype(F32) + image_own
    grad_image = grad_image + dot(sel, grad_back[pl.ds(96, 128), :], ((0,), (0,)))
    top = grad_back[pl.ds(48, 48), :].astype(F32)
    bottom = grad_back[pl.ds(0, 48), :].astype(F32)
    grad_image = jnp.concatenate(
        [grad_image[:48] + top, grad_image[48:80], grad_image[80:] + bottom], axis=0
    )
    grad_image_ref[...] = grad_image.astype(BF16)

    start_gather()
    cast(spot, CAST_SEM, CASTS_FIRST, NZ)

    @pl.when(chip == 0)
    def _():
        @pl.when(z < OWNER_PLANES)
        def _():
            wait_received(small_line.at[pl.ds(0, NZ - 1)], SMALL_LINE)
            line = small_line[0]
            for k in range(1, NZ):
                line = line + small_line[k]
            small_total[...] = line * factor

        cast(small_total, SMALL_CAST, 0, CASTS_FIRST)

        @pl.when(z >= OWNER_PLANES)
        def _():
            wait_received(small_total, SMALL_CAST)

        for other, device in peers:
            remote(small_total, small_total, SMALL_GATHER, device).start()

        cast(small_total, SMALL_CAST, CASTS_FIRST, NZ)

    wait_received(gathered.at[0, pl.ds(0, NP - 1)], GATHER_SEM)
    remote(own_half, own_half, BOTH_SEM, sibling).start()

    @pl.when(core == 0)
    def _():
        deliver_half(0)

    @pl.when(core == 1)
    def _():
        deliver_half(1)

    @pl.when(chip != 0)
    def _():
        wait_received(small_total, SMALL_GATHER)

    wait_received(gathered.at[1 - core], BOTH_SEM)

    @pl.when(core == 0)
    def _():
        deliver_half(1)

    @pl.when(core == 1)
    def _():
        deliver_half(0)

    wait_sent(halo, HALO_SEM)
    wait_sent(grad_send, BACK_SEM)
    wait_sent(small_own, SMALL_CORE)
    wait_sent(gathered.at[0, pl.ds(0, NP - 1)], GATHER_SEM)
    wait_sent(own_half, BOTH_SEM)
    for stage in range(2):
        wait_sent(core_send.at[stage], CORE_SEM + stage)
        wait_sent(plane_recv.at[stage], PLANE_SEM + stage)

    @pl.when(z >= OWNER_PLANES)
    def _():
        for stage in range(2):
            wait_sent(line_recv.at[stage, pl.ds(0, OWNER_PLANES)], LINE_SEM + stage)

    @pl.when(z < OWNER_PLANES)
    def _():
        for stage in range(2):
            wait_sent(line_send.at[stage], LINE_SEM + stage)

    for owner in range(OWNER_PLANES):

        @pl.when(z == owner)
        def _():
            wait_sent(gathered.at[0, pl.ds(0, len(CASTS[owner]))], CAST_SEM)

    @pl.when(chip != 0)
    def _():
        wait_sent(small_total, SMALL_PLANE)

    @pl.when(chip == 0)
    def _():
        wait_sent(small_plane.at[pl.ds(0, NP - 1)], SMALL_GATHER)

        @pl.when(z >= OWNER_PLANES)
        def _():
            wait_sent(small_line.at[pl.ds(0, OWNER_PLANES)], SMALL_LINE)

        @pl.when(z < OWNER_PLANES)
        def _():
            wait_sent(small_total, SMALL_LINE)

        for owner in range(OWNER_PLANES):

            @pl.when(z == owner)
            def _():
                wait_sent(small_line.at[pl.ds(0, len(CASTS[owner]))], SMALL_CAST)


def deliver(
    output,
    grad_image,
    grad_qkv,
    grad_out,
    small,
    output_out,
    grad_image_out,
    grad_qkv_out,
    grad_out_out,
    gain_out,
    scale_out,
    gain_ref,
    scale_ref,
    sems,
):
    steps = (
        (grad_qkv, grad_qkv_out),
        (grad_out, grad_out_out),
        (output, output_out),
        (grad_image, grad_image_out),
        (gain_ref, gain_out),
        (scale_ref, scale_out),
    )
    copies = [pltpu.make_async_copy(a, b, sems.at[i]) for i, (a, b) in enumerate(steps)]
    for copy in copies[:4]:
        copy.start()
    gain_ref[:, pl.ds(0, OWN)] = small[pl.ds(1, 1), :]
    gain_ref[:, pl.ds(OWN, OWN)] = small[pl.ds(2, 1), :]
    scale_ref[...] = small[pl.ds(0, 1), pl.ds(0, HEADS)]
    for copy in copies[4:]:
        copy.start()
    for copy in copies:
        copy.wait()


def on_device(image, w_qkv, w_out, norm_gain, head_scale, cotangent):
    rows = lax.axis_size("row")
    cols = lax.axis_size("col")
    vmem = pl.BlockSpec(memory_space=pltpu.VMEM)
    hbm = pl.BlockSpec(memory_space=pl.ANY)
    factor = 1.0 / math.sqrt(rows * TH * cols * TW)

    def kernel(*refs):
        block(rows, cols, factor, *refs)

    def pinned(array):
        return pltpu.with_memory_space_constraint(array, pltpu.HBM)

    parts = pl.pallas_call(
        kernel,
        out_shape=(
            pltpu.VMEM((OWN, C), BF16),
            pltpu.VMEM((OWN, C), BF16),
            pltpu.VMEM((C, 3 * C), F32),
            pltpu.VMEM((C, C), F32),
            pltpu.VMEM((8, OWN), F32),
        ),
        in_specs=[hbm] * 6,
        out_specs=(vmem,) * 5,
        scratch_shapes=[
            pltpu.VMEM((OWN, C), BF16),
            pltpu.VMEM((C, 3 * C), BF16),
            pltpu.VMEM((C, C), BF16),
            pltpu.VMEM((1, C), F32),
            pltpu.SMEM((1, HEADS), F32),
            pltpu.VMEM((OWN, C), BF16),
            pltpu.VMEM((HALO, C), BF16),
            pltpu.VMEM((OWN, C), BF16),
            pltpu.VMEM((HALO, C), BF16),
            pltpu.VMEM((HALO, C), BF16),
            pltpu.VMEM((C, LANES), BF16),
            pltpu.VMEM((C, LANES), BF16),
            pltpu.VMEM((4, C, C), F32),
            pltpu.VMEM((2, C, C), BF16),
            pltpu.VMEM((2, C, C), BF16),
            pltpu.VMEM((2, C, C), F32),
            pltpu.VMEM((2, C, C), BF16),
            pltpu.VMEM((2, NP - 1, 16, C), BF16),
            pltpu.VMEM((2, 16, C), BF16),
            pltpu.VMEM((2, NZ, 16, C), BF16),
            pltpu.VMEM((2, NP, 2, 16, C), BF16),
            pltpu.VMEM((8, OWN), F32),
            pltpu.VMEM((8, OWN), F32),
            pltpu.VMEM((NP, 8, OWN), F32),
            pltpu.VMEM((NZ, 8, OWN), F32),
            pltpu.SemaphoreType.DMA((32,)),
            pltpu.SemaphoreType.DMA((6,)),
        ],
        compiler_params=pltpu.CompilerParams(
            collective_id=0, has_side_effects=True, vmem_limit_bytes=VMEM_LIMIT
        ),
    )(
        *map(
            pinned,
            (
                image.reshape(OWN, C),
                w_qkv,
                w_out,
                norm_gain.reshape(1, C),
                head_scale.reshape(1, HEADS),
                cotangent.reshape(OWN, C),
            ),
        )
    )
    output, grad_image, grad_qkv, grad_out, grad_gain, grad_scale = pl.pallas_call(
        deliver,
        out_shape=(
            jax.ShapeDtypeStruct((OWN, C), BF16),
            jax.ShapeDtypeStruct((OWN, C), BF16),
            jax.ShapeDtypeStruct((C, 3 * C), F32),
            jax.ShapeDtypeStruct((C, C), F32),
            jax.ShapeDtypeStruct((1, C), F32),
            jax.ShapeDtypeStruct((1, HEADS), F32),
        ),
        in_specs=[vmem] * 5,
        out_specs=(hbm,) * 6,
        scratch_shapes=[
            pltpu.VMEM((1, C), F32),
            pltpu.VMEM((1, HEADS), F32),
            pltpu.SemaphoreType.DMA((6,)),
        ],
        compiler_params=pltpu.CompilerParams(vmem_limit_bytes=VMEM_LIMIT),
    )(*(pltpu.with_memory_space_constraint(part, pltpu.VMEM) for part in parts))
    return (
        output.reshape(TH, TW, C),
        grad_image.reshape(TH, TW, C),
        grad_qkv,
        grad_out,
        grad_gain.reshape(C),
        grad_scale.reshape(HEADS),
    )


def solution(mesh):
    placed = (P("row", "col", None), P(), P(), P(), P(), P("row", "col", None))
    return jax.shard_map(
        on_device,
        mesh=mesh,
        in_specs=placed,
        out_specs=(P("row", "col", None), P("row", "col", None), P(), P(), P(), P()),
        check_vma=False,
    )
```
